128 devices in a mesh: sweep: 32 (over z, x, core), grp: 4 (over y).
Axes of the slice: x: 4, y: 4, z: 4, core: 2. Of those that a mesh axis runs over, the one named last changes fastest.
Arguments:
- state: float32 [4, 128, 6, 4096], P('grp', 'sweep'), may hold values from -6 to 6
- forcing: float32 [4, 128, 6, 4096], P('grp', 'sweep'), may hold values from -6 to 6
- viscosity: float32 [4, 128, 4096], P('grp', 'sweep'), may hold values from 0.05 to 0.5
- inverses: float32 [4, 128, 6, 6], P('grp', 'sweep'), as said below
- lower_jac: float32 [4, 128, 6, 6], P('grp', 'sweep')
- upper_jac: float32 [4, 128, 6, 6], P('grp', 'sweep')
- diag_scale: float32 [4, 128, 4096], P('grp', 'sweep'), may hold values from 0.99 to 1
- lower_coupling: float32 [4, 128, 4096], P('grp', 'sweep'), may hold values from 0.3 to 1
- upper_coupling: float32 [4, 128, 4096], P('grp', 'sweep'), may hold values from 0.3 to 1
- donor_block: int32 [128, 128, 32], P(('sweep', 'grp')), may hold values from 0 to 3
- donor_point: int32 [128, 128, 32], P(('sweep', 'grp')), may hold values from 0 to 4092
- donor_weight: float32 [128, 128, 32, 4], P(('sweep', 'grp')), may hold values from 0.1 to 1
- fringe_block: int32 [128, 128, 32], P(('sweep', 'grp')), may hold values from 0 to 3
- fringe_point: int32 [128, 128, 32], P(('sweep', 'grp')), may hold values from 0 to 4095
- block_order: int32 [4, 128], P('grp', 'sweep'), may hold values from 0 to 3, as said below
Outputs:
- new_state: float32 [4, 128, 6, 4096], P('grp', 'sweep')
- correction: float32 [4, 128, 6, 4096], P('grp', 'sweep')
The draws below stay inside these ranges and needn't reach their ends.
Inputs may be any that keep to these rules, and one draw needn't show every extreme that they name: `block_order`: each device's 4 consecutive entries of a lane are a permutation of 0 to 3. `inverses`: diagonally dominant.
All inputs are finite; a program needn't handle non-finite values.
Results may differ from the reference program's by a relative error of at most 0.0003.
Values sent between devices are 32-bit elements; how exact they have to be, the bound alone decides.
No kernel may reach another device: no remote copies, remote signals or barrier semaphores. Data moves between devices by JAX's collectives and lax.ppermute only.
A program may use at most 64 MiB of HBM per device.

```python
import math
import jax
import jax.numpy as jnp
from jax import lax

VARS = 6
STENCIL = 4
STEPS = 2
BLK_DEV = 4
PTS = 4096
SLOTS = 32
BLOCK_CHAINS = 4
NBLK = 128
N_GRP = 4
DEVICES = 128


def draw_block_order(key, part):
    key = jax.random.fold_in(key, 1)
    count = BLOCK_CHAINS * NBLK // BLK_DEV
    keys = jax.random.split(key, count)
    perms = jax.vmap(lambda one: jax.random.permutation(one, BLK_DEV))(keys)
    return perms.reshape(BLOCK_CHAINS, NBLK).astype(jnp.int32)


def inverse_diagonal(key):
    key = jax.random.fold_in(key, 17)
    return jnp.exp(jax.random.uniform(key, (BLOCK_CHAINS, NBLK, VARS), jnp.float32, jnp.log(0.001), jnp.log(0.003)))


def draw_inverses(key, part):
    diag = inverse_diagonal(key)
    key = jax.random.fold_in(key, 2)
    shape = (BLOCK_CHAINS, NBLK, VARS, VARS)
    rel = jnp.clip(0.0001 * jax.random.normal(key, shape, jnp.float32), -0.0002, 0.0002)
    eye = jnp.eye(VARS, dtype=jnp.float32)
    return diag[..., None] * (eye + rel * (1.0 - eye))


def jacobian_from(key, diag, fast_share, slow_lo, slow_hi):
    first, second, third_factor, fourth = jax.random.split(key, 4)
    shape = (BLOCK_CHAINS, NBLK, VARS)
    fast = jax.random.uniform(first, (BLOCK_CHAINS, 1, VARS), jnp.float32) < fast_share
    slow_gain = jnp.exp(jax.random.uniform(second, shape, jnp.float32, jnp.log(slow_lo), jnp.log(slow_hi)))
    fast_gain = jnp.exp(jax.random.uniform(third_factor, shape, jnp.float32, jnp.log(0.2), jnp.log(0.5)))
    gain = jnp.where(fast, fast_gain, slow_gain)
    rel = jax.random.uniform(fourth, shape + (VARS,), jnp.float32, -0.0002, 0.0002)
    eye = jnp.eye(VARS, dtype=jnp.float32)
    return (gain / diag)[..., None] * (eye + rel * (1.0 - eye))


def draw_lower_jac(key, part):
    diag = inverse_diagonal(key)
    key = jax.random.fold_in(key, 3)
    return jacobian_from(key, diag, 0.4, 0.992, 0.996)


def draw_upper_jac(key, part):
    diag = inverse_diagonal(key)
    key = jax.random.fold_in(key, 4)
    return jacobian_from(key, diag, 0.4, 0.992, 0.996)


def source_coupling(key, baseline_lower, spike_lower, spike_upper):
    first, second, third_factor = jax.random.split(key, 3)
    base = jnp.exp(jax.random.uniform(first, (BLOCK_CHAINS, NBLK, PTS), jnp.float32, jnp.log(baseline_lower), 0.0))
    places = jax.random.randint(second, (BLOCK_CHAINS, 2), 0, NBLK)
    coupling_magnitude = jax.random.uniform(third_factor, (BLOCK_CHAINS, 2), jnp.float32, spike_lower, spike_upper)
    blocks = jnp.arange(NBLK, dtype=jnp.int32)[None, :, None]
    struck = blocks == places[:, None, :]
    factor = jnp.prod(jnp.where(struck, coupling_magnitude[:, None, :], 1.0), axis=2)
    return base * factor[..., None]


def draw_lower_coupling(key, part):
    key = jax.random.fold_in(key, 5)
    return source_coupling(key, 0.998, 0.55, 0.8)


def draw_upper_coupling(key, part):
    key = jax.random.fold_in(key, 6)
    return source_coupling(key, 0.998, 0.55, 0.8)


def with_ends(drawn, key, least, top_value):
    shape = drawn.shape
    spot = [jax.random.randint(jax.random.fold_in(key, axis), (), 0, shape[axis]) for axis in range(len(shape))]
    drawn = drawn.at[tuple(spot)].set(least)
    longest = shape.index(max(shape))
    spot[longest] = (spot[longest] + 1) % shape[longest]
    return drawn.at[tuple(spot)].set(top_value)


def level_of(rng, extent, cuts, low, high):
    def one(dim, parts):
        draws = jax.random.uniform(jax.random.fold_in(jax.random.fold_in(rng, 6), dim), (parts,), jnp.float32, low / len(cuts), high / len(cuts))
        return jnp.repeat(jnp.exp(draws), extent[dim] // parts).reshape((-1,) + (1,) * (len(extent) - dim - 1))

    level = one(*cuts[0])
    for cut in cuts[1:]:
        level = level * one(*cut)
    return level


def centred(stream_key, shape, scale, limit, cuts=(), kind=jnp.bfloat16):
    entries = scale * jax.random.normal(stream_key, shape, jnp.float32)
    if cuts:
        entries = entries * level_of(stream_key, shape, cuts, -0.22, 0.18)
    return jnp.clip(entries, -limit, limit).astype(kind)


def setup_inputs(seed: int = 0) -> dict:
    arg_keys = jax.random.split(jax.random.key(seed), 16)
    return {
        "state": centred(arg_keys[0], (BLOCK_CHAINS, NBLK, VARS, PTS), 1.0, 6.0, ((0, 4), (1, 32)), jnp.float32),
        "forcing": centred(arg_keys[1], (BLOCK_CHAINS, NBLK, VARS, PTS), 1.0, 6.0, ((0, 4), (1, 32)), jnp.float32),
        "viscosity": jnp.clip(jnp.exp(math.log(0.5) - 2.3025851 * jax.random.uniform(arg_keys[2], (BLOCK_CHAINS, NBLK, PTS), jnp.float32) ** level_of(arg_keys[2], (BLOCK_CHAINS, NBLK, PTS), ((0, 4), (1, 32)), -0.2, 0.2)), 0.05, 0.5),
        "inverses": draw_inverses(jax.random.fold_in(arg_keys[15], 71), 0),
        "lower_jac": draw_lower_jac(jax.random.fold_in(arg_keys[15], 71), 0),
        "upper_jac": draw_upper_jac(jax.random.fold_in(arg_keys[15], 71), 0),
        "diag_scale": jnp.clip(jnp.exp(math.log(1.0) - 0.0100503262 * jax.random.uniform(arg_keys[6], (BLOCK_CHAINS, NBLK, PTS), jnp.float32) ** level_of(arg_keys[6], (BLOCK_CHAINS, NBLK, PTS), ((0, 4), (1, 32)), -0.2, 0.2)), 0.99, 1.0),
        "lower_coupling": draw_lower_coupling(jax.random.fold_in(arg_keys[15], 71), 0),
        "upper_coupling": draw_upper_coupling(jax.random.fold_in(arg_keys[15], 71), 0),
        "donor_block": with_ends(jax.random.randint(arg_keys[9], (DEVICES, DEVICES, SLOTS), 0, BLK_DEV), jax.random.fold_in(arg_keys[9], 1), 0, BLK_DEV - 1).astype(jnp.int32),
        "donor_point": with_ends(jax.random.randint(arg_keys[10], (DEVICES, DEVICES, SLOTS), 0, PTS - STENCIL + 1), jax.random.fold_in(arg_keys[10], 1), 0, PTS - STENCIL).astype(jnp.int32),
        "donor_weight": jnp.clip(jnp.exp(math.log(1.0) - 2.3025851 * jax.random.uniform(arg_keys[11], (DEVICES, DEVICES, SLOTS, STENCIL), jnp.float32) ** level_of(arg_keys[11], (DEVICES, DEVICES, SLOTS, STENCIL), ((0, 128),), -0.2, 0.2)), 0.1, 1.0),
        "fringe_block": with_ends(jax.random.randint(arg_keys[12], (DEVICES, DEVICES, SLOTS), 0, BLK_DEV), jax.random.fold_in(arg_keys[12], 1), 0, BLK_DEV - 1).astype(jnp.int32),
        "fringe_point": with_ends(jax.random.randint(arg_keys[13], (DEVICES, DEVICES, SLOTS), 0, PTS), jax.random.fold_in(arg_keys[13], 1), 0, PTS - 1).astype(jnp.int32),
        "block_order": draw_block_order(jax.random.fold_in(arg_keys[15], 71), 0),
    }


def second_diff(field, viscosity):
    padded = jnp.pad(field, ((0, 0), (0, 0), (0, 0), (1, 1)))
    return viscosity[:, :, None, :] * (padded[..., 2:] - 2.0 * field + padded[..., :-2])


def sweep_lane(gmats, factor, offset, reverse):
    def advance(carry, items):
        gmat, scale, base = items
        nxt = scale[:, None, :] * jnp.einsum("lij,ljp->lip", gmat, carry, precision=lax.Precision.HIGHEST) + base
        return nxt, nxt
    start = jnp.zeros_like(offset[:, 0])
    items = (jnp.swapaxes(gmats, 0, 1), jnp.swapaxes(factor, 0, 1), jnp.swapaxes(offset, 0, 1))
    _, values = lax.scan(advance, start, items, reverse=reverse)
    return jnp.swapaxes(values, 0, 1)


def reference(state, forcing, viscosity, inverses, lower_jac, upper_jac, diag_scale, lower_coupling, upper_coupling, donor_block, donor_point, donor_weight, fringe_block, fringe_point, block_order):
    devs = jnp.arange(DEVICES, dtype=jnp.int32)
    lane_of = devs % N_GRP
    base_of = (devs // N_GRP) * BLK_DEV
    seq = (jnp.arange(NBLK, dtype=jnp.int32) // BLK_DEV)[None, :] * BLK_DEV + block_order
    lanes_col = jnp.arange(BLOCK_CHAINS, dtype=jnp.int32)[:, None]
    hi = lax.Precision.HIGHEST
    g_low = jnp.einsum("lbij,lbjk->lbik", inverses, lower_jac, precision=hi)
    g_up = jnp.einsum("lbij,lbjk->lbik", inverses, upper_jac, precision=hi)
    g_low_p = jnp.take_along_axis(g_low, seq[:, :, None, None], 1)
    g_up_p = jnp.take_along_axis(g_up, seq[:, :, None, None], 1)
    low_factor = jnp.take_along_axis(diag_scale * lower_coupling, seq[:, :, None], 1)
    up_factor = jnp.take_along_axis(upper_coupling, seq[:, :, None], 1)
    src_lane = jnp.broadcast_to(lane_of[:, None, None, None], donor_point.shape + (STENCIL,))
    src_blk = jnp.broadcast_to((base_of[:, None, None] + donor_block)[..., None], donor_point.shape + (STENCIL,))
    src_pt = donor_point[..., None] + jnp.arange(STENCIL, dtype=jnp.int32)
    dst_lane = jnp.broadcast_to(lane_of[:, None, None], fringe_block.shape)
    dst_blk = base_of[:, None, None] + fringe_block
    state_now = state
    correction = jnp.zeros_like(state)
    for step in range(STEPS):
        samples = state_now[src_lane, src_blk, :, src_pt]
        interp = jnp.sum(donor_weight[..., None] * samples, axis=3)
        values = jnp.swapaxes(interp, 0, 1)
        residual = forcing + second_diff(state_now, viscosity)
        residual = residual.at[dst_lane, dst_blk, :, fringe_point].add(values - state_now[dst_lane, dst_blk, :, fringe_point])
        solved = diag_scale[:, :, None, :] * jnp.einsum("lbij,lbjp->lbip", inverses, residual, precision=hi)
        solved_p = jnp.take_along_axis(solved, seq[:, :, None, None], 1)
        star = sweep_lane(g_low_p, low_factor, solved_p, False)
        corr_p = sweep_lane(g_up_p, up_factor, star, True)
        correction = jnp.zeros_like(state).at[lanes_col, seq].set(corr_p)
        state_now = state_now + correction
    return state_now, correction
```

```python
import jax
import jax.numpy as jnp
from jax import lax
from jax.experimental import pallas as pl
from jax.experimental.pallas import tpu as pltpu
from jax.sharding import PartitionSpec as P

F32 = jnp.float32
BF16 = jnp.bfloat16
VARS = 6
BLK = 4
TILES = 32
SLOTS = 32
LANES = 128
HALF = 64
TAIL = 8
GROUP = 4
VMEM = pl.BlockSpec(memory_space=pltpu.VMEM)
SMEM = pl.BlockSpec(memory_space=pltpu.SMEM)
PARAMS = pltpu.CompilerParams(vmem_limit_bytes=40 * 1024 * 1024)


def to_rows(x):
    return x.reshape(BLK, VARS, TILES, LANES).transpose(1, 2, 0, 3).reshape(VARS, TILES * BLK, LANES)


def from_rows(x):
    return x.reshape(VARS, TILES, BLK, LANES).transpose(2, 0, 1, 3).reshape(BLK, VARS, TILES * LANES)


def field_rows(x):
    return x.reshape(BLK, TILES, LANES).transpose(1, 0, 2).reshape(TILES * BLK, LANES)


def one_hot(count, index):
    places = lax.broadcasted_iota(jnp.int32, (count, index.shape[1]), 0)
    return jnp.where(places == index, 1.0, 0.0).astype(BF16)


def window_of(block, point):
    return ((point >> 6) & 1) * LANES + (point >> 7) * BLK + block


def split(x):
    high = x.astype(BF16)
    return high, (x - high.astype(F32)).astype(BF16)


def interpolate(state_ref, block_ref, point_ref, weight_ref, out_ref, high_ref, low_ref, acc_ref):
    tails = []
    for v in range(VARS):
        turned = state_ref[v].T
        main = jnp.concatenate([turned[:HALF], turned[HALF:]], axis=1)
        high, low = split(main)
        high_ref[v * HALF : (v + 1) * HALF] = high
        low_ref[v * HALF : (v + 1) * HALF] = low
        following = pltpu.roll(turned[:TAIL], LANES - BLK, 1)
        tails.append(jnp.concatenate([turned[HALF : HALF + TAIL], following], axis=1))
    high, low = split(jnp.concatenate(tails, axis=0))
    high_ref[VARS * HALF :] = high
    low_ref[VARS * HALF :] = low
    acc_ref[VARS * SLOTS :] = jnp.zeros((256 - VARS * SLOTS, LANES), F32)
    for first in range(0, SLOTS, GROUP):
        picks, weights = [], []
        for c in range(first, first + GROUP):
            point = point_ref[c : c + 1]
            picks.append(one_hot(256, window_of(block_ref[c : c + 1], point)))
            ahead = lax.broadcasted_iota(jnp.int32, (HALF + TAIL, LANES), 0) - (point & (HALF - 1))
            row = jnp.zeros((HALF + TAIL, LANES), F32)
            for j in range(4):
                row = jnp.where(ahead == j, weight_ref[c, j : j + 1], row)
            weights.append(row)
        pick = jnp.concatenate(picks, axis=1)
        found = jnp.dot(high_ref[...], pick, preferred_element_type=F32)
        found = found + jnp.dot(low_ref[...], pick, preferred_element_type=F32)
        for n, row in enumerate(weights):
            cols = slice(n * LANES, (n + 1) * LANES)
            for v in range(VARS):
                main = found[v * HALF : (v + 1) * HALF, cols] * row[:HALF]
                start = VARS * HALF + v * TAIL
                tail = found[start : start + TAIL, cols] * row[HALF:]
                total = jnp.sum(main, axis=0, keepdims=True) + jnp.sum(tail, axis=0, keepdims=True)
                acc_ref[v * SLOTS + first + n : v * SLOTS + first + n + 1] = total
    out_ref[pl.ds(0, LANES, stride=2), :] = acc_ref[:LANES].T
    out_ref[pl.ds(1, LANES, stride=2), :] = acc_ref[LANES:].T


def product(a, b):
    total = a[:, 0:1] * b[0:1, :]
    for j in range(1, VARS):
        total = total + a[:, j : j + 1] * b[j : j + 1, :]
    return total


def matrices(inv_ref, low_jac_ref, up_jac_ref, order_ref, low_ref, up_ref, mats_ref, square_ref):
    for which, (jac_ref, out_ref) in enumerate(((low_jac_ref, low_ref), (up_jac_ref, up_ref))):
        for i in range(VARS):
            row = inv_ref[i]
            total = row[:, 0:1] * jac_ref[0]
            for j in range(1, VARS):
                total = total + row[:, j : j + 1] * jac_ref[j]
            out_ref[i] = total
        for k in range(BLK):
            for i in range(VARS):
                square_ref[which * BLK + k, i : i + 1, :] = out_ref[i, pl.ds(order_ref[0, k], 1), :]
    low = [square_ref[k] for k in range(BLK)]
    up = [square_ref[BLK + k] for k in range(BLK)]
    downs = [low[0]]
    for k in range(1, BLK):
        downs.append(product(low[k], downs[-1]))
    ups = [up[0]]
    for k in range(1, BLK):
        ups.append(product(ups[-1], up[k]))
    mixed = [downs[0]] + [product(ups[k - 1], downs[k]) for k in range(1, BLK)]
    mats_ref[...] = jnp.zeros_like(mats_ref)
    for m, mat in enumerate([downs[-1], ups[-1]] + mixed):
        mats_ref[0:VARS, m * VARS : (m + 1) * VARS] = mat


def first_kernel(
    state_ref, block_ref, point_ref, weight_ref, inv_ref, low_jac_ref, up_jac_ref, order_ref,
    out_ref, low_ref, up_ref, mats_ref, high_s, low_s, acc_s, square_s,
):
    matrices(inv_ref, low_jac_ref, up_jac_ref, order_ref, low_ref, up_ref, mats_ref, square_s)
    interpolate(state_ref, block_ref, point_ref, weight_ref, out_ref, high_s, low_s, acc_s)


def scatter(got_ref, block_ref, point_ref, added_ref, count_ref, high_s, low_s, left_s, right_s, total_s, counting):
    got = jnp.concatenate(
        [got_ref[pl.ds(0, LANES, stride=2), :].T, got_ref[pl.ds(1, LANES, stride=2), :].T[: VARS * SLOTS - LANES]], axis=0
    )
    high = got.astype(BF16).astype(F32)
    high_s[...] = high
    low_s[...] = got - high
    size = VARS * HALF
    for c in range(SLOTS):
        cols = slice(c * LANES, (c + 1) * LANES)
        point = point_ref[c : c + 1]
        right_s[:, cols] = one_hot(256, window_of(block_ref[c : c + 1], point))
        here = lax.broadcasted_iota(jnp.int32, (HALF, LANES), 0) == (point & (HALF - 1))
        for v in range(VARS):
            row = v * SLOTS + c
            left_s[v * HALF : (v + 1) * HALF, cols] = jnp.where(here, high_s[row : row + 1], 0.0).astype(BF16)
            left_s[size + v * HALF : size + (v + 1) * HALF, cols] = jnp.where(here, low_s[row : row + 1], 0.0).astype(BF16)
        if counting:
            left_s[2 * size :, cols] = jnp.where(here, 1.0, 0.0).astype(BF16)
    total_s[...] = lax.dot_general(left_s[...], right_s[...], (((1,), (1,)), ((), ())), preferred_element_type=F32)

    def turned(x):
        return jnp.concatenate([x[:, :LANES], x[:, LANES:]], axis=0).T

    for v in range(VARS):
        first = total_s[v * HALF : (v + 1) * HALF]
        added_ref[v] = turned(first + total_s[size + v * HALF : size + (v + 1) * HALF])
    if counting:
        count_ref[...] = turned(total_s[2 * size :])


def apply_block(mat_ref, b, xs):
    out = []
    for i in range(VARS):
        total = mat_ref[i, b, 0] * xs[0]
        for j in range(1, VARS):
            total = total + mat_ref[i, b, j] * xs[j]
        out.append(total)
    return out


SPAN = 16


def pick(ref, b, first):
    return ref[pl.ds(b + BLK * first, SPAN, stride=BLK), :]


def solve_kernel(counting, rows, *refs):
    (
        got_ref, block_ref, point_ref, state_ref, forcing_ref, visc_ref, diag_ref, lowc_ref, upc_ref,
        inv_ref, low_ref, up_ref, order_ref, extra_ref,
    ) = refs[:14]
    if counting:
        chunk_ref, z_ref, count_ref = refs[14:17]
        scratch = refs[17:]
    else:
        chunk_ref, z_ref = refs[14:16]
        count_ref = extra_ref
        scratch = refs[16:]
    resid_s, high_s, low_s, left_s, right_s, total_s = scratch
    scatter(got_ref, block_ref, point_ref, resid_s, count_ref, high_s, low_s, left_s, right_s, total_s, counting)
    lane = lax.broadcasted_iota(jnp.int32, (LANES, LANES), 1)
    row = lax.broadcasted_iota(jnp.int32, (LANES, LANES), 0)
    for v in range(VARS):
        x = state_ref[v]
        after = pltpu.roll(x, LANES - 1, 1)
        after = jnp.where(lane == LANES - 1, pltpu.roll(after, LANES - BLK, 0), after)
        after = jnp.where((lane == LANES - 1) & (row >= LANES - BLK), 0.0, after)
        before = pltpu.roll(x, 1, 1)
        before = jnp.where(lane == 0, pltpu.roll(before, BLK, 0), before)
        before = jnp.where((lane == 0) & (row < BLK), 0.0, before)
        flux = visc_ref[...] * (after - 2.0 * x + before)
        resid_s[v] = forcing_ref[v] + flux + (resid_s[v] - count_ref[...] * x)
    if counting:
        for s in range(TILES):
            chunk_ref[s * rows + 16 : s * rows + 24] = extra_ref[...]
    for first in range(0, TILES, SPAN):

        def put(r, value):
            chunk_ref[pl.ds(first * rows + r, SPAN, stride=rows), :] = value

        z, stars, factors = None, [], []
        for k in range(BLK):
            b = order_ref[0, k]
            scale = pick(diag_ref, b, first)
            solved = apply_block(inv_ref, b, [pick(resid_s.at[j], b, first) for j in range(VARS)])
            factor = scale * pick(lowc_ref, b, first)
            if k == 0:
                z = [scale * x for x in solved]
            else:
                moved = apply_block(low_ref, b, z)
                z = [factor * m + scale * x for m, x in zip(moved, solved)]
            for i in range(VARS):
                z_ref[k, i, first : first + SPAN] = z[i]
            factors.append(factor)
        for i in range(VARS):
            put(i, z[i])
        y = z
        for k in reversed(range(BLK - 1)):
            b = order_ref[0, k]
            moved = apply_block(up_ref, b, y)
            factor = pick(upc_ref, b, first)
            y = [z_ref[k, i, first : first + SPAN] + factor * moved[i] for i in range(VARS)]
        for i in range(VARS):
            put(8 + i, y[i])
        if counting:
            down, up = factors[0], pick(upc_ref, order_ref[0, 0], first)
            places = (14, 15, 22, 23)
            put(places[0], down)
            for k in range(1, BLK):
                down = down * factors[k]
                put(places[k], down * up)
                up = up * pick(upc_ref, order_ref[0, k], first)
            put(6, down)
            put(7, up)
        else:
            for r in (6, 7, 14, 15):
                put(r, jnp.zeros((SPAN, LANES), F32))


def chain_kernel(rows, in_ref, coef_ref, out_ref, mid_s):
    def column(tile, m, j):
        at = m * VARS + j
        return jnp.broadcast_to(tile[:, at : at + 1], (8, LANES))

    def spread(x):
        return [jnp.broadcast_to(x[j : j + 1], (8, LANES)) for j in range(VARS)]

    def apply(tile, m, parts):
        terms = [column(tile, m, j) * parts[j] for j in range(VARS)]
        return ((terms[0] + terms[1]) + (terms[2] + terms[3])) + (terms[4] + terms[5])

    count = TILES
    down = jnp.zeros((8, LANES), F32)
    for s in range(count):
        out_ref[16 * s : 16 * s + 8] = down
        tile = coef_ref[24 * s + 16 : 24 * s + 24]
        parts = spread(down)
        mid = in_ref[rows * s + 8 : rows * s + 16]
        for k, place in enumerate((14, 15, 22, 23)):
            mid = mid + coef_ref[24 * s + place : 24 * s + place + 1] * apply(tile, 2 + k, parts)
        mid_s[s] = mid
        down = coef_ref[24 * s + 6 : 24 * s + 7] * apply(tile, 0, parts) + in_ref[rows * s : rows * s + 8]
    up = jnp.zeros((8, LANES), F32)
    for s in reversed(range(count)):
        out_ref[16 * s + 8 : 16 * s + 16] = up
        tile = coef_ref[24 * s + 16 : 24 * s + 24]
        up = coef_ref[24 * s + 7 : 24 * s + 8] * apply(tile, 1, spread(up)) + mid_s[s]


def finish(back_ref, z_ref, state_ref, diag_ref, lowc_ref, upc_ref, low_ref, up_ref, order_ref, new_ref, corr_ref, star_s):
    for first in range(0, TILES, SPAN):
        enter = [back_ref[pl.ds(first * 16 + i, SPAN, stride=16), :] for i in range(VARS)]
        for k in range(BLK):
            b = order_ref[0, k]
            factor = pick(diag_ref, b, first) * pick(lowc_ref, b, first)
            enter = [factor * m for m in apply_block(low_ref, b, enter)]
            for i in range(VARS):
                star_s[k, i, first : first + SPAN] = enter[i] + z_ref[k, i, first : first + SPAN]
        corr = [back_ref[pl.ds(first * 16 + 8 + i, SPAN, stride=16), :] for i in range(VARS)]
        for k in reversed(range(BLK)):
            b = order_ref[0, k]
            factor = pick(upc_ref, b, first)
            moved = apply_block(up_ref, b, corr)
            corr = [star_s[k, i, first : first + SPAN] + factor * moved[i] for i in range(VARS)]
            for i in range(VARS):
                rows = pl.ds(b + BLK * first, SPAN, stride=BLK)
                if corr_ref is not None:
                    corr_ref[i, rows, :] = corr[i]
                new_ref[i, rows, :] = state_ref[i, rows, :] + corr[i]


def middle_kernel(
    back_ref, z_ref, state_ref, diag_ref, lowc_ref, upc_ref, low_ref, up_ref, order_ref,
    block_ref, point_ref, weight_ref, new_ref, out_ref, star_s, high_s, low_s, acc_s,
):
    finish(back_ref, z_ref, state_ref, diag_ref, lowc_ref, upc_ref, low_ref, up_ref, order_ref, new_ref, None, star_s)
    interpolate(new_ref, block_ref, point_ref, weight_ref, out_ref, high_s, low_s, acc_s)


def shape(*dims):
    return jax.ShapeDtypeStruct(dims, F32)


def per_device(
    state, forcing, viscosity, inverses, lower_jac, upper_jac, diag_scale, lower_coupling, upper_coupling,
    donor_block, donor_point, donor_weight, fringe_block, fringe_point, block_order,
):
    big = (VARS, TILES * BLK, LANES)
    state, forcing = to_rows(state[0]), to_rows(forcing[0])
    visc, diag, lowc, upc = (field_rows(x[0]) for x in (viscosity, diag_scale, lower_coupling, upper_coupling))
    inv, low_jac, up_jac = (x[0].transpose(1, 0, 2) for x in (inverses, lower_jac, upper_jac))
    src_block, src_point, dst_block, dst_point = (x[0].T for x in (donor_block, donor_point, fringe_block, fringe_point))
    weight = donor_weight[0].transpose(1, 2, 0)
    sent = VARS * (HALF + TAIL)
    gather_scratch = [pltpu.VMEM((sent, 256), BF16), pltpu.VMEM((sent, 256), BF16), pltpu.VMEM((256, LANES), F32)]

    interp, low, up, mats = pl.pallas_call(
        first_kernel,
        out_shape=[shape(256, LANES), shape(VARS, BLK, VARS), shape(VARS, BLK, VARS), shape(8, LANES)],
        in_specs=[VMEM] * 7 + [SMEM],
        out_specs=[VMEM] * 4,
        scratch_shapes=gather_scratch + [pltpu.VMEM((2 * BLK, VARS, VARS), F32)],
        compiler_params=PARAMS,
        name="first",
    )(state, src_block, src_point, weight, inv, low_jac, up_jac, block_order)

    def exchange(x, axes, count):
        parts = x.reshape(count, -1, LANES)
        return lax.all_to_all(parts, axes, split_axis=0, concat_axis=0, tiled=True).reshape(x.shape)

    def solve(counting, got, state, extra):
        rows = 24 if counting else 16
        left = (2 * VARS + counting) * HALF
        outs = [shape(TILES * rows, LANES), shape(BLK, VARS, TILES, LANES)] + [shape(LANES, LANES)] * counting
        return pl.pallas_call(
            lambda *refs: solve_kernel(counting, rows, *refs),
            out_shape=outs,
            in_specs=[VMEM] * 9 + [SMEM] * 4 + [VMEM],
            out_specs=[VMEM] * len(outs),
            scratch_shapes=[
                pltpu.VMEM(big, F32),
                pltpu.VMEM((VARS * SLOTS, LANES), F32),
                pltpu.VMEM((VARS * SLOTS, LANES), F32),
                pltpu.VMEM((left, SLOTS * LANES), BF16),
                pltpu.VMEM((256, SLOTS * LANES), BF16),
                pltpu.VMEM((left, 256), F32),
            ],
            compiler_params=PARAMS,
            name="solve",
        )(got, dst_block, dst_point, state, forcing, visc, diag, lowc, upc, inv, low, up, block_order, extra)

    def chain(values, coefs):
        return pl.pallas_call(
            lambda *refs: chain_kernel(values.shape[0] // TILES, *refs),
            out_shape=shape(TILES * 16, LANES),
            in_specs=[VMEM] * 2,
            out_specs=VMEM,
            scratch_shapes=[pltpu.VMEM((TILES, 8, LANES), F32)],
            compiler_params=PARAMS,
            name="chain",
        )(values, coefs)

    got = exchange(interp, ("sweep", "grp"), 128)
    chunk, z, count = solve(True, got, state, mats)
    coefs = exchange(chunk, "sweep", TILES)
    back = exchange(chain(coefs, coefs), "sweep", TILES)
    star_scratch = pltpu.VMEM((BLK, VARS, TILES, LANES), F32)
    state, interp = pl.pallas_call(
        middle_kernel,
        out_shape=[shape(*big), shape(256, LANES)],
        in_specs=[VMEM] * 6 + [SMEM] * 3 + [VMEM] * 3,
        out_specs=[VMEM] * 2,
        scratch_shapes=[star_scratch] + gather_scratch,
        compiler_params=PARAMS,
        name="middle",
    )(back, z, state, diag, lowc, upc, low, up, block_order, src_block, src_point, weight)
    got = exchange(interp, ("sweep", "grp"), 128)
    chunk, z = solve(False, got, state, count)
    back = exchange(chain(exchange(chunk, "sweep", TILES), coefs), "sweep", TILES)
    state, correction = pl.pallas_call(
        finish,
        out_shape=[shape(*big), shape(*big)],
        in_specs=[VMEM] * 6 + [SMEM] * 3,
        out_specs=[VMEM] * 2,
        scratch_shapes=[star_scratch],
        compiler_params=PARAMS,
        name="finish",
    )(back, z, state, diag, lowc, upc, low, up, block_order)
    return from_rows(state)[None], from_rows(correction)[None]


def solution(mesh):
    blocks = P("grp", "sweep", None, None)
    field = P("grp", "sweep", None)
    table = P(("sweep", "grp"), None, None)
    return jax.shard_map(
        per_device,
        mesh=mesh,
        in_specs=(
            blocks, blocks, field, blocks, blocks, blocks, field, field, field,
            table, table, P(("sweep", "grp"), None, None, None), table, table, P("grp", "sweep"),
        ),
        out_specs=(blocks, blocks),
        check_vma=False,
    )
```

```python
import jax
import jax.numpy as jnp
from jax import lax
from jax.experimental import pallas as pl
from jax.experimental.pallas import tpu as pltpu
from jax.sharding import PartitionSpec as P

F32 = jnp.float32
BF16 = jnp.bfloat16
VARS = 6
BLK = 4
TILES = 32
SLOTS = 32
LANES = 128
ROWS = TILES * BLK
HALF = 64
TAIL = 8
GROUP = 4
BATCH = 8
SPAN = 16
SQUARE = VARS * VARS
INV, LOW, UP = 0, 1, 2
DIAG, DOWN, RISE = 0, 1, 2
FULL = 20
BARE = 12
VMEM = pl.BlockSpec(memory_space=pltpu.VMEM)
PARAMS = pltpu.CompilerParams(vmem_limit_bytes=24 * 1024 * 1024)
BESIDE = pl.CostEstimate(flops=20_000_000_000, bytes_accessed=4_000_000, transcendentals=0)


def to_rows(x):
    return x.reshape(BLK, VARS, TILES, LANES).transpose(1, 2, 0, 3).reshape(VARS, ROWS, LANES)


def from_rows(x):
    return x.reshape(VARS, TILES, BLK, LANES).transpose(2, 0, 1, 3).reshape(BLK, VARS, TILES * LANES)


def field_rows(x):
    return x.reshape(BLK, TILES, LANES).transpose(1, 0, 2).reshape(ROWS, LANES)


def one_hot(count, index):
    places = lax.broadcasted_iota(jnp.int32, (count, index.shape[1]), 0)
    return jnp.where(places == index, 1.0, 0.0).astype(BF16)


def window_of(block, point):
    return ((point >> 6) & 1) * LANES + (point >> 7) * BLK + block


def split(x):
    high = x.astype(BF16)
    return high, (x - high.astype(F32)).astype(BF16)


def order_of(order_ref):
    order = order_ref[...]
    return [order[0, k] for k in range(BLK)]


def windows(state_ref, high_ref, low_ref):
    tails = []
    for v in range(VARS):
        turned = state_ref[v].T
        high, low = split(jnp.concatenate([turned[:HALF], turned[HALF:]], axis=1))
        high_ref[v * HALF : (v + 1) * HALF] = high
        low_ref[v * HALF : (v + 1) * HALF] = low
        following = pltpu.roll(turned[:TAIL], LANES - BLK, 1)
        tails.append(jnp.concatenate([turned[HALF : HALF + TAIL], following], axis=1))
    high, low = split(jnp.concatenate(tails, axis=0))
    high_ref[VARS * HALF :] = high
    low_ref[VARS * HALF :] = low


def stencil_of(point, weight_ref, c):
    ahead = lax.broadcasted_iota(jnp.int32, (HALF + TAIL, LANES), 0) - (point & (HALF - 1))
    row = jnp.zeros((HALF + TAIL, LANES), F32)
    for j in range(4):
        row = jnp.where(ahead == j, weight_ref[c, j : j + 1], row)
    return row


def gather(block_ref, point_ref, weight_ref, out_ref, high_ref, low_ref, acc_ref):
    acc_ref[VARS * SLOTS :] = jnp.zeros((256 - VARS * SLOTS, LANES), F32)
    for first in range(0, SLOTS, GROUP):
        picks = []
        for c in range(first, first + GROUP):
            picks.append(one_hot(256, window_of(block_ref[c : c + 1], point_ref[c : c + 1])))
        pick = jnp.concatenate(picks, axis=1)
        found = jnp.dot(high_ref[...], pick, preferred_element_type=F32)
        found = found + jnp.dot(low_ref[...], pick, preferred_element_type=F32)
        for n in range(GROUP):
            cols = slice(n * LANES, (n + 1) * LANES)
            row = stencil_of(point_ref[first + n : first + n + 1], weight_ref, first + n)
            for v in range(VARS):
                main = found[v * HALF : (v + 1) * HALF, cols] * row[:HALF]
                start = VARS * HALF + v * TAIL
                tail = found[start : start + TAIL, cols] * row[HALF:]
                total = jnp.sum(main, axis=0, keepdims=True) + jnp.sum(tail, axis=0, keepdims=True)
                acc_ref[v * SLOTS + first + n : v * SLOTS + first + n + 1] = total
    out_ref[pl.ds(0, LANES, stride=2), :] = acc_ref[:LANES].T
    out_ref[pl.ds(1, LANES, stride=2), :] = acc_ref[LANES:].T


def fetch(pairs, sems):
    copies = [pltpu.make_async_copy(src, dst, sems.at[n]) for n, (src, dst) in enumerate(pairs)]
    for copy in copies:
        copy.start()
    return copies


def first_kernel(
    block_hbm, point_hbm, state_hbm, weight_hbm, out_ref, state_ref, block_s, point_s, weight_s, high_s, low_s, acc_s, sems
):
    pairs = ((block_hbm, block_s), (point_hbm, point_s), (state_hbm, state_ref), (weight_hbm, weight_s))
    for copy in fetch(pairs, sems):
        copy.wait()
    windows(state_ref, high_s, low_s)
    gather(block_s, point_s, weight_s, out_ref, high_s, low_s, acc_s)


def product(a, b):
    total = a[:, 0:1] * b[0:1, :]
    for j in range(1, VARS):
        total = total + a[:, j : j + 1] * b[j : j + 1, :]
    return total


def matrices(inv_ref, low_jac_ref, up_jac_ref, order, wide_ref, maps_ref, native_s, square_s, spread_s, mats_s):
    for i in range(VARS):
        row = inv_ref[i]
        native_s[INV, i] = row
        for which, jac_ref in ((LOW, low_jac_ref), (UP, up_jac_ref)):
            total = row[:, 0:1] * jac_ref[0]
            for j in range(1, VARS):
                total = total + row[:, j : j + 1] * jac_ref[j]
            native_s[which, i] = total
    for which in (INV, LOW, UP):
        for i in range(VARS):
            row = native_s[which, i]
            for j in range(VARS):
                at = ((which * VARS + i) * VARS + j) * BLK
                spread_s[at : at + BLK] = jnp.broadcast_to(row[:, j : j + 1], (BLK, LANES))
    for k in range(BLK):
        wide_ref[k] = spread_s[pl.ds(order[k], 3 * SQUARE, stride=BLK), :]
        for which in (LOW, UP):
            for i in range(VARS):
                square_s[which * BLK + k, i : i + 1, :] = native_s[which, i, pl.ds(order[k], 1), :]
    low = [square_s[LOW * BLK + k] for k in range(BLK)]
    up = [square_s[UP * BLK + k] for k in range(BLK)]
    downs, ups = [low[0]], [up[0]]
    for k in range(1, BLK):
        downs.append(product(low[k], downs[-1]))
        ups.append(product(ups[-1], up[k]))
    mixed = [downs[0]] + [product(ups[k - 1], downs[k]) for k in range(1, BLK)]
    mats_s[...] = jnp.zeros_like(mats_s)
    for m, mat in enumerate([downs[-1], ups[-1]] + mixed):
        mats_s[0:VARS, m * VARS : (m + 1) * VARS] = mat
    mats = mats_s[...]
    for half in range(2):
        line = mats[3 * half : 3 * half + 1]
        for n in (1, 2):
            line = line + pltpu.roll(mats[3 * half + n : 3 * half + n + 1], n * SQUARE, 1)
        maps_ref[6 + half] = jnp.broadcast_to(line, (TILES, LANES))


def residual(state_ref, forcing_ref, visc_ref, count_ref, out_ref):
    count = count_ref[...]
    lane = lax.broadcasted_iota(jnp.int32, (ROWS, LANES), 1)
    row = lax.broadcasted_iota(jnp.int32, (ROWS, LANES), 0)
    for v in range(VARS):
        x = state_ref[v]
        after = pltpu.roll(x, LANES - 1, 1)
        after = jnp.where(lane == LANES - 1, pltpu.roll(after, ROWS - BLK, 0), after)
        after = jnp.where((lane == LANES - 1) & (row >= ROWS - BLK), 0.0, after)
        before = pltpu.roll(x, 1, 1)
        before = jnp.where(lane == 0, pltpu.roll(before, BLK, 0), before)
        before = jnp.where((lane == 0) & (row < BLK), 0.0, before)
        out_ref[v] = forcing_ref[v] + visc_ref[...] * (after - 2.0 * x + before) + (out_ref[v] - count * x)


def turned(x):
    return jnp.concatenate([x[:, :LANES], x[:, LANES:]], axis=0).T


def contract(left, right):
    return lax.dot_general(left, right, (((1,), (1,)), ((), ())), preferred_element_type=F32)


def base_kernel(
    block_hbm, point_hbm, diag_hbm, lowc_hbm, upc_hbm, inv_hbm, low_jac_hbm, up_jac_hbm, order_hbm,
    place_ref, count_ref, wide_ref, factor_ref, maps_ref, point_ref, order_ref,
    block_ref, diag_ref, lowc_ref, upc_ref, inv_ref, low_jac_ref, up_jac_ref,
    left_s, native_s, square_s, spread_s, mats_s, sems,
):
    pairs = (
        (block_hbm, block_ref), (point_hbm, point_ref), (order_hbm, order_ref), (inv_hbm, inv_ref),
        (low_jac_hbm, low_jac_ref), (up_jac_hbm, up_jac_ref), (diag_hbm, diag_ref), (lowc_hbm, lowc_ref),
        (upc_hbm, upc_ref),
    )
    for copy in fetch(pairs, sems):
        copy.wait()
    order = order_of(order_ref)
    for c in range(SLOTS):
        cols = slice(c * LANES, (c + 1) * LANES)
        point = point_ref[c : c + 1]
        place_ref[:, cols] = one_hot(256, window_of(block_ref[c : c + 1], point))
        left_s[:, cols] = one_hot(HALF, point & (HALF - 1))
    matrices(inv_ref, low_jac_ref, up_jac_ref, order, wide_ref, maps_ref, native_s, square_s, spread_s, mats_s)
    down = up = None
    for k in range(BLK):
        rows = pl.ds(order[k], TILES, stride=BLK)
        scale = diag_ref[rows, :]
        fall, rise = scale * lowc_ref[rows, :], upc_ref[rows, :]
        factor_ref[DIAG * BLK + k] = scale
        factor_ref[DOWN * BLK + k] = fall
        factor_ref[RISE * BLK + k] = rise
        down = fall if k == 0 else down * fall
        maps_ref[2 + k] = down if k == 0 else down * up
        up = rise if k == 0 else up * rise
    maps_ref[0] = down
    maps_ref[1] = up
    count_ref[...] = turned(contract(left_s[...], place_ref[...]))


def scatter(got_ref, point_ref, place_ref, out_ref, high_s, low_s, total_s):
    high_s[:LANES] = got_ref[pl.ds(0, LANES, stride=2), :].T
    high_s[LANES:] = got_ref[pl.ds(1, LANES, stride=2), :].T[: VARS * SLOTS - LANES]
    got = high_s[...]
    high = got.astype(BF16).astype(F32)
    high_s[...] = high
    low_s[...] = got - high
    for first in range(0, SLOTS, BATCH):
        parts = []
        for c in range(first, first + BATCH):
            here = lax.broadcasted_iota(jnp.int32, (HALF, LANES), 0) == (point_ref[c : c + 1] & (HALF - 1))
            pieces = []
            for ref in (high_s, low_s):
                for v in range(VARS):
                    pieces.append(jnp.where(here, ref[v * SLOTS + c : v * SLOTS + c + 1], 0.0).astype(BF16))
            parts.append(jnp.concatenate(pieces, axis=0))
        left = jnp.concatenate(parts, axis=1)
        total = contract(left, place_ref[:, first * LANES : (first + BATCH) * LANES])
        if first == 0:
            total_s[...] = total
        else:
            total_s[...] += total
    size = VARS * HALF
    for v in range(VARS):
        added = total_s[v * HALF : (v + 1) * HALF] + total_s[size + v * HALF : size + (v + 1) * HALF]
        out_ref[v] = turned(added)


def apply_block(wide_ref, k, which, xs):
    out = []
    for i in range(VARS):
        at = which * SQUARE + i * VARS
        total = wide_ref[k, at : at + 1] * xs[0]
        for j in range(1, VARS):
            total = total + wide_ref[k, at + j : at + j + 1] * xs[j]
        out.append(total)
    return out


def factor_at(factor_ref, which, k, first):
    return factor_ref[which * BLK + k, first : first + SPAN]


def solve_kernel(full, *refs):
    rows = FULL if full else BARE
    got_ref, point_ref, place_ref, wide_ref, factor_ref, order_ref, count_ref, state_ref, visc_hbm, forcing_hbm = refs[:10]
    refs = refs[10:]
    if full:
        maps_ref, refs = refs[0], refs[1:]
    chunk_ref, z_ref, resid_s, high_s, low_s, total_s, visc_s, forcing_s, sems = refs
    copies = fetch(((visc_hbm, visc_s), (forcing_hbm, forcing_s)), sems)
    order = order_of(order_ref)
    scatter(got_ref, point_ref, place_ref, resid_s, high_s, low_s, total_s)
    for copy in copies:
        copy.wait()
    residual(state_ref, forcing_s, visc_s, count_ref, resid_s)
    if full:
        for r in range(FULL - BARE):
            chunk_ref[pl.ds(BARE + r, TILES, stride=rows), :] = maps_ref[r]
    for first in range(0, TILES, SPAN):

        def put(r, value):
            chunk_ref[pl.ds(first * rows + r, SPAN, stride=rows), :] = value

        z = None
        for k in range(BLK):
            places = pl.ds(order[k] + BLK * first, SPAN, stride=BLK)
            scale = factor_at(factor_ref, DIAG, k, first)
            solved = [scale * x for x in apply_block(wide_ref, k, INV, [resid_s[j, places, :] for j in range(VARS)])]
            if k > 0:
                fall = factor_at(factor_ref, DOWN, k, first)
                solved = [fall * m + x for m, x in zip(apply_block(wide_ref, k, LOW, z), solved)]
            z = solved
            for i in range(VARS):
                z_ref[k, i, first : first + SPAN] = z[i]
        for i in range(VARS):
            put(i, z[i])
        y = z
        for k in reversed(range(BLK - 1)):
            rise = factor_at(factor_ref, RISE, k, first)
            moved = apply_block(wide_ref, k, UP, y)
            y = [z_ref[k, i, first : first + SPAN] + rise * moved[i] for i in range(VARS)]
        for i in range(VARS):
            put(VARS + i, y[i])


def chain_kernel(rows, in_ref, coef_ref, out_ref, value_s, mid_s, mats_s):
    for half in range(2):
        lines = coef_ref[pl.ds(FULL - 2 + half, TILES, stride=FULL), :]
        for n in range(3):
            shifted = pltpu.roll(lines, LANES - n * SQUARE, 1) if n else lines
            mats_s[pl.ds(3 * half + n, TILES, stride=8), :] = shifted
        for i in range(VARS):
            to = value_s if half == 0 else mid_s
            to[pl.ds(i, TILES, stride=8), :] = in_ref[pl.ds(half * VARS + i, TILES, stride=rows), :]

    def apply(mats, m, x):
        terms = []
        for j in range(VARS):
            at = m * VARS + j
            column = jnp.broadcast_to(mats[:, at : at + 1], (VARS, LANES))
            terms.append(column * x[j])
        return ((terms[0] + terms[1]) + (terms[2] + terms[3])) + (terms[4] + terms[5])

    def spread(x):
        return [jnp.broadcast_to(x[j : j + 1], (VARS, LANES)) for j in range(VARS)]

    def coef(s, r):
        return coef_ref[FULL * s + BARE + r : FULL * s + BARE + r + 1]

    down = jnp.zeros((VARS, LANES), F32)
    for s in range(TILES):
        here = slice(8 * s, 8 * s + VARS)
        mats = mats_s[here]
        parts = spread(down)
        mid = mid_s[here]
        for k in range(BLK):
            mid = mid + coef(s, 2 + k) * apply(mats, 2 + k, parts)
        mid_s[here] = mid
        after = coef(s, 0) * apply(mats, 0, parts) + value_s[here]
        value_s[here] = down
        down = after
    up = jnp.zeros((VARS, LANES), F32)
    for s in reversed(range(TILES)):
        here = slice(8 * s, 8 * s + VARS)
        after = coef(s, 1) * apply(mats_s[here], 1, spread(up)) + mid_s[here]
        mid_s[here] = up
        up = after
    for i in range(VARS):
        out_ref[pl.ds(i, TILES, stride=BARE), :] = value_s[pl.ds(i, TILES, stride=8), :]
        out_ref[pl.ds(VARS + i, TILES, stride=BARE), :] = mid_s[pl.ds(i, TILES, stride=8), :]


def finish(back_ref, z_ref, state_ref, wide_ref, factor_ref, order_ref, new_ref, corr_ref, star_s):
    order = order_of(order_ref)
    for first in range(0, TILES, SPAN):
        here = slice(first, first + SPAN)
        enter = [back_ref[pl.ds(first * BARE + i, SPAN, stride=BARE), :] for i in range(VARS)]
        for k in range(BLK):
            fall = factor_at(factor_ref, DOWN, k, first)
            enter = [fall * m for m in apply_block(wide_ref, k, LOW, enter)]
            for i in range(VARS):
                star_s[k, i, here] = enter[i] + z_ref[k, i, here]
        corr = [back_ref[pl.ds(first * BARE + VARS + i, SPAN, stride=BARE), :] for i in range(VARS)]
        for k in reversed(range(BLK)):
            rise = factor_at(factor_ref, RISE, k, first)
            moved = apply_block(wide_ref, k, UP, corr)
            corr = [star_s[k, i, here] + rise * moved[i] for i in range(VARS)]
            places = pl.ds(order[k] + BLK * first, SPAN, stride=BLK)
            for i in range(VARS):
                if corr_ref is not None:
                    corr_ref[i, places, :] = corr[i]
                new_ref[i, places, :] = state_ref[i, places, :] + corr[i]


def middle_kernel(
    back_ref, z_ref, state_ref, wide_ref, factor_ref, order_ref, block_hbm, point_hbm, weight_hbm, new_ref, out_ref,
    star_s, block_s, point_s, weight_s, high_s, low_s, acc_s, sems,
):
    copies = fetch(((block_hbm, block_s), (point_hbm, point_s), (weight_hbm, weight_s)), sems)
    finish(back_ref, z_ref, state_ref, wide_ref, factor_ref, order_ref, new_ref, None, star_s)
    windows(new_ref, high_s, low_s)
    for copy in copies:
        copy.wait()
    gather(block_s, point_s, weight_s, out_ref, high_s, low_s, acc_s)


def shape(*dims, dtype=F32):
    return pltpu.VMEM(dims, dtype)


def call(kernel, name, outs, operands, scratch=(), outside=(), beside=False):
    spaces = [pltpu.HBM if n in outside else pltpu.VMEM for n in range(len(operands))]
    return pl.pallas_call(
        kernel,
        out_shape=outs,
        in_specs=[pl.BlockSpec(memory_space=space) for space in spaces],
        out_specs=[VMEM] * len(outs),
        scratch_shapes=list(scratch),
        compiler_params=PARAMS,
        cost_estimate=BESIDE if beside else None,
        name=name,
    )(*[pltpu.with_memory_space_constraint(x, pltpu.HBM) if n in outside else x for n, x in enumerate(operands)])


def exchange(x, axes, count):
    parts = x.reshape(count, 1, -1)
    return lax.all_to_all(parts, axes, split_axis=0, concat_axis=0, tiled=True).reshape(x.shape)


def per_device(
    state, forcing, viscosity, inverses, lower_jac, upper_jac, diag_scale, lower_coupling, upper_coupling,
    donor_block, donor_point, donor_weight, fringe_block, fringe_point, block_order,
):
    big = (VARS, ROWS, LANES)
    state, forcing = to_rows(state[0]), to_rows(forcing[0])
    visc, diag, lowc, upc = (field_rows(x[0]) for x in (viscosity, diag_scale, lower_coupling, upper_coupling))
    inv, low_jac, up_jac = (x[0].transpose(1, 0, 2) for x in (inverses, lower_jac, upper_jac))
    src_block, src_point, dst_block, dst_point = (x[0].T for x in (donor_block, donor_point, fringe_block, fringe_point))
    weight = donor_weight[0].transpose(1, 2, 0)
    sent = VARS * (HALF + TAIL)
    gather_scratch = [pltpu.VMEM((sent, 256), BF16), pltpu.VMEM((sent, 256), BF16), pltpu.VMEM((256, LANES), F32)]
    star_scratch = [pltpu.VMEM((BLK, VARS, TILES, LANES), F32)]
    chain_scratch = [pltpu.VMEM((TILES * 8, LANES), F32) for _ in range(3)]
    dma = pltpu.SemaphoreType.DMA

    def alike(x):
        return pltpu.VMEM(x.shape, x.dtype)

    source = (src_block, src_point, weight)
    source_scratch = [alike(x) for x in source] + gather_scratch
    solve_scratch = [
        pltpu.VMEM(big, F32),
        pltpu.VMEM((VARS * SLOTS, LANES), F32),
        pltpu.VMEM((VARS * SLOTS, LANES), F32),
        pltpu.VMEM((2 * VARS * HALF, 256), F32),
        alike(visc),
        alike(forcing),
        dma((2,)),
    ]
    interp, state = call(
        first_kernel,
        "first",
        [shape(256, LANES), shape(*big)],
        (src_block, src_point, state, weight),
        source_scratch + [dma((4,))],
        outside=range(4),
    )
    got = exchange(interp, ("sweep", "grp"), 128)
    place, count, wide, factors, maps, dst_point, block_order = call(
        base_kernel,
        "base",
        [
            shape(256, SLOTS * LANES, dtype=BF16),
            shape(ROWS, LANES),
            shape(BLK, 3 * SQUARE, LANES),
            shape(3 * BLK, TILES, LANES),
            shape(FULL - BARE, TILES, LANES),
            alike(dst_point),
            alike(block_order),
        ],
        (dst_block, dst_point, diag, lowc, upc, inv, low_jac, up_jac, block_order),
        [alike(x) for x in (dst_block, diag, lowc, upc, inv, low_jac, up_jac)]
        + [
            pltpu.VMEM((HALF, SLOTS * LANES), BF16),
            pltpu.VMEM((3, VARS, BLK, VARS), F32),
            pltpu.VMEM((3 * BLK, VARS, VARS), F32),
            pltpu.VMEM((3 * SQUARE * BLK, LANES), F32),
            pltpu.VMEM((8, LANES), F32),
            dma((9,)),
        ],
        outside=range(9),
        beside=True,
    )

    def solve(full, got, state):
        operands = (got, dst_point, place, wide, factors, block_order, count, state, visc, forcing)
        operands += (maps,) if full else ()
        rows = FULL if full else BARE
        outs = [shape(TILES * rows, LANES), shape(BLK, VARS, TILES, LANES)]
        return call(lambda *refs: solve_kernel(full, *refs), "solve", outs, operands, solve_scratch, outside=(8, 9))

    def chain(values, coefs):
        rows = values.shape[0] // TILES
        outs = [shape(TILES * BARE, LANES)]
        return call(lambda *refs: chain_kernel(rows, *refs), "chain", outs, (values, coefs), chain_scratch)[0]

    chunk, z = solve(True, got, state)
    coefs = exchange(chunk, "sweep", TILES)
    back = exchange(chain(coefs, coefs), "sweep", TILES)
    state, interp = call(
        middle_kernel,
        "middle",
        [shape(*big), shape(256, LANES)],
        (back, z, state, wide, factors, block_order) + source,
        star_scratch + source_scratch + [dma((3,))],
        outside=(6, 7, 8),
    )
    got = exchange(interp, ("sweep", "grp"), 128)
    chunk, z = solve(False, got, state)
    back = exchange(chain(exchange(chunk, "sweep", TILES), coefs), "sweep", TILES)
    state, correction = call(
        finish, "finish", [jax.ShapeDtypeStruct(big, F32)] * 2, (back, z, state, wide, factors, block_order), star_scratch
    )
    return from_rows(state)[None], from_rows(correction)[None]


def solution(mesh):
    blocks = P("grp", "sweep", None, None)
    field = P("grp", "sweep", None)
    table = P(("sweep", "grp"), None, None)
    return jax.shard_map(
        per_device,
        mesh=mesh,
        in_specs=(
            blocks, blocks, field, blocks, blocks, blocks, field, field, field,
            table, table, P(("sweep", "grp"), None, None, None), table, table, P("grp", "sweep"),
        ),
        out_specs=(blocks, blocks),
        check_vma=False,
    )
```

```python
import jax
import jax.numpy as jnp
from jax import lax
from jax.experimental import pallas as pl
from jax.experimental.pallas import tpu as pltpu
from jax.sharding import PartitionSpec as P

F32 = jnp.float32
BF16 = jnp.bfloat16
VARS = 6
BLK = 4
TILES = 32
SLOTS = 32
LANES = 128
ROWS = TILES * BLK
HALF = 64
TAIL = 8
GROUP = 4
BATCH = 8
SPAN = 16
SQUARE = VARS * VARS
INV, LOW, UP = 0, 1, 2
DIAG, DOWN, RISE = 0, 1, 2
FULL = 20
BARE = 12
VMEM = pl.BlockSpec(memory_space=pltpu.VMEM)
PARAMS = pltpu.CompilerParams(vmem_limit_bytes=24 * 1024 * 1024)
BESIDE = pl.CostEstimate(flops=20_000_000_000, bytes_accessed=4_000_000, transcendentals=0)


def to_rows(x):
    return x.reshape(BLK, VARS, TILES, LANES).transpose(1, 2, 0, 3).reshape(VARS, ROWS, LANES)


def from_rows(x):
    return x.reshape(VARS, TILES, BLK, LANES).transpose(2, 0, 1, 3).reshape(BLK, VARS, TILES * LANES)


def field_rows(x):
    return x.reshape(BLK, TILES, LANES).transpose(1, 0, 2).reshape(ROWS, LANES)


def one_hot(count, index):
    size = (count, index.shape[1])
    places = lax.broadcasted_iota(jnp.int32, size, 0).astype(F32).astype(BF16)
    index = jnp.broadcast_to(index.astype(F32), size).astype(BF16)
    return jnp.where(places == index, jnp.ones((), BF16), jnp.zeros((), BF16))


def window_of(block, point):
    return ((point >> 6) & 1) * LANES + (point >> 7) * BLK + block


def split(x):
    high = x.astype(BF16)
    return high, (x - high.astype(F32)).astype(BF16)


def order_of(order_ref):
    order = order_ref[...]
    return [order[0, k] for k in range(BLK)]


def windows(state_ref, high_ref, low_ref):
    tails = []
    for v in range(VARS):
        turned = state_ref[v].T
        high, low = split(jnp.concatenate([turned[:HALF], turned[HALF:]], axis=1))
        high_ref[v * HALF : (v + 1) * HALF] = high
        low_ref[v * HALF : (v + 1) * HALF] = low
        following = pltpu.roll(turned[:TAIL], LANES - BLK, 1)
        tails.append(jnp.concatenate([turned[HALF : HALF + TAIL], following], axis=1))
    high, low = split(jnp.concatenate(tails, axis=0))
    high_ref[VARS * HALF :] = high
    low_ref[VARS * HALF :] = low


def stencil_of(point, weight_ref, c):
    ahead = lax.broadcasted_iota(jnp.int32, (HALF + TAIL, LANES), 0) - (point & (HALF - 1))
    row = jnp.zeros((HALF + TAIL, LANES), F32)
    for j in range(4):
        row = jnp.where(ahead == j, weight_ref[c, j : j + 1], row)
    return row


def picks(block_ref, point_ref, pick_ref):
    for c in range(SLOTS):
        window = window_of(block_ref[c : c + 1], point_ref[c : c + 1])
        pick_ref[:, c * LANES : (c + 1) * LANES] = one_hot(256, window)


def gather(pick_ref, point_ref, weight_ref, out_ref, high_ref, low_ref, acc_ref):
    acc_ref[VARS * SLOTS :] = jnp.zeros((256 - VARS * SLOTS, LANES), F32)
    for first in range(0, SLOTS, GROUP):
        pick = pick_ref[:, first * LANES : (first + GROUP) * LANES]
        found = jnp.dot(high_ref[...], pick, preferred_element_type=F32)
        found = found + jnp.dot(low_ref[...], pick, preferred_element_type=F32)
        for n in range(GROUP):
            cols = slice(n * LANES, (n + 1) * LANES)
            row = stencil_of(point_ref[first + n : first + n + 1], weight_ref, first + n)
            for v in range(VARS):
                main = found[v * HALF : (v + 1) * HALF, cols] * row[:HALF]
                start = VARS * HALF + v * TAIL
                tail = found[start : start + TAIL, cols] * row[HALF:]
                total = jnp.sum(main, axis=0, keepdims=True) + jnp.sum(tail, axis=0, keepdims=True)
                acc_ref[v * SLOTS + first + n : v * SLOTS + first + n + 1] = total
    out_ref[pl.ds(0, LANES, stride=2), :] = acc_ref[:LANES].T
    out_ref[pl.ds(1, LANES, stride=2), :] = acc_ref[LANES:].T


def fetch(pairs, sems):
    copies = [pltpu.make_async_copy(src, dst, sems.at[n]) for n, (src, dst) in enumerate(pairs)]
    for copy in copies:
        copy.start()
    return copies


def first_kernel(
    block_hbm, point_hbm, state_hbm, weight_hbm, out_ref, state_ref,
    block_s, point_s, weight_s, pick_s, high_s, low_s, acc_s, sems,
):
    pairs = ((block_hbm, block_s), (point_hbm, point_s), (state_hbm, state_ref), (weight_hbm, weight_s))
    copies = fetch(pairs, sems)
    copies[0].wait()
    copies[1].wait()
    picks(block_s, point_s, pick_s)
    copies[2].wait()
    windows(state_ref, high_s, low_s)
    copies[3].wait()
    gather(pick_s, point_s, weight_s, out_ref, high_s, low_s, acc_s)


def product(a, b):
    total = a[:, 0:1] * b[0:1, :]
    for j in range(1, VARS):
        total = total + a[:, j : j + 1] * b[j : j + 1, :]
    return total


def matrices(inv_ref, low_jac_ref, up_jac_ref, order, wide_ref, maps_ref, native_s, square_s, spread_s, mats_s):
    for i in range(VARS):
        row = inv_ref[i]
        native_s[INV, i] = row
        for which, jac_ref in ((LOW, low_jac_ref), (UP, up_jac_ref)):
            total = row[:, 0:1] * jac_ref[0]
            for j in range(1, VARS):
                total = total + row[:, j : j + 1] * jac_ref[j]
            native_s[which, i] = total
    for which in (INV, LOW, UP):
        for i in range(VARS):
            row = native_s[which, i]
            for j in range(VARS):
                at = ((which * VARS + i) * VARS + j) * BLK
                spread_s[at : at + BLK] = jnp.broadcast_to(row[:, j : j + 1], (BLK, LANES))
    for k in range(BLK):
        wide_ref[k] = spread_s[pl.ds(order[k], 3 * SQUARE, stride=BLK), :]
        for which in (LOW, UP):
            for i in range(VARS):
                square_s[which * BLK + k, i : i + 1, :] = native_s[which, i, pl.ds(order[k], 1), :]
    low = [square_s[LOW * BLK + k] for k in range(BLK)]
    up = [square_s[UP * BLK + k] for k in range(BLK)]
    downs, ups = [low[0]], [up[0]]
    for k in range(1, BLK):
        downs.append(product(low[k], downs[-1]))
        ups.append(product(ups[-1], up[k]))
    mixed = [downs[0]] + [product(ups[k - 1], downs[k]) for k in range(1, BLK)]
    mats_s[...] = jnp.zeros_like(mats_s)
    for m, mat in enumerate([downs[-1], ups[-1]] + mixed):
        mats_s[0:VARS, m * VARS : (m + 1) * VARS] = mat
    mats = mats_s[...]
    for half in range(2):
        line = mats[3 * half : 3 * half + 1]
        for n in (1, 2):
            line = line + pltpu.roll(mats[3 * half + n : 3 * half + n + 1], n * SQUARE, 1)
        maps_ref[6 + half] = jnp.broadcast_to(line, (TILES, LANES))


def residual(state_ref, forcing_ref, visc_ref, count_ref, out_ref):
    count = count_ref[...]
    lane = lax.broadcasted_iota(jnp.int32, (ROWS, LANES), 1)
    row = lax.broadcasted_iota(jnp.int32, (ROWS, LANES), 0)
    for v in range(VARS):
        x = state_ref[v]
        after = pltpu.roll(x, LANES - 1, 1)
        after = jnp.where(lane == LANES - 1, pltpu.roll(after, ROWS - BLK, 0), after)
        after = jnp.where((lane == LANES - 1) & (row >= ROWS - BLK), 0.0, after)
        before = pltpu.roll(x, 1, 1)
        before = jnp.where(lane == 0, pltpu.roll(before, BLK, 0), before)
        before = jnp.where((lane == 0) & (row < BLK), 0.0, before)
        out_ref[v] = forcing_ref[v] + visc_ref[...] * (after - 2.0 * x + before) + (out_ref[v] - count * x)


def turned(x):
    return jnp.concatenate([x[:, :LANES], x[:, LANES:]], axis=0).T


def contract(left, right):
    return lax.dot_general(left, right, (((1,), (1,)), ((), ())), preferred_element_type=F32)


def base_kernel(
    block_hbm, point_hbm, diag_hbm, lowc_hbm, upc_hbm, inv_hbm, low_jac_hbm, up_jac_hbm, order_hbm,
    place_ref, count_ref, wide_ref, factor_ref, maps_ref, point_ref, order_ref,
    block_ref, diag_ref, lowc_ref, upc_ref, inv_ref, low_jac_ref, up_jac_ref,
    left_s, native_s, square_s, spread_s, mats_s, sems,
):
    pairs = (
        (block_hbm, block_ref), (point_hbm, point_ref), (order_hbm, order_ref), (inv_hbm, inv_ref),
        (low_jac_hbm, low_jac_ref), (up_jac_hbm, up_jac_ref), (diag_hbm, diag_ref), (lowc_hbm, lowc_ref),
        (upc_hbm, upc_ref),
    )
    for copy in fetch(pairs, sems):
        copy.wait()
    order = order_of(order_ref)
    for c in range(SLOTS):
        cols = slice(c * LANES, (c + 1) * LANES)
        point = point_ref[c : c + 1]
        place_ref[:, cols] = one_hot(256, window_of(block_ref[c : c + 1], point))
        left_s[:, cols] = one_hot(HALF, point & (HALF - 1))
    matrices(inv_ref, low_jac_ref, up_jac_ref, order, wide_ref, maps_ref, native_s, square_s, spread_s, mats_s)
    down = up = None
    for k in range(BLK):
        rows = pl.ds(order[k], TILES, stride=BLK)
        scale = diag_ref[rows, :]
        fall, rise = scale * lowc_ref[rows, :], upc_ref[rows, :]
        factor_ref[DIAG * BLK + k] = scale
        factor_ref[DOWN * BLK + k] = fall
        factor_ref[RISE * BLK + k] = rise
        down = fall if k == 0 else down * fall
        maps_ref[2 + k] = down if k == 0 else down * up
        up = rise if k == 0 else up * rise
    maps_ref[0] = down
    maps_ref[1] = up
    count_ref[...] = turned(contract(left_s[...], place_ref[...]))


def scatter(got_ref, point_ref, place_ref, out_ref, high_s, low_s, total_s):
    high_s[:LANES] = got_ref[pl.ds(0, LANES, stride=2), :].T
    high_s[LANES:] = got_ref[pl.ds(1, LANES, stride=2), :].T[: VARS * SLOTS - LANES]
    got = high_s[...]
    high = got.astype(BF16).astype(F32)
    high_s[...] = high
    low_s[...] = got - high
    for first in range(0, SLOTS, BATCH):
        parts = []
        for c in range(first, first + BATCH):
            here = lax.broadcasted_iota(jnp.int32, (HALF, LANES), 0) == (point_ref[c : c + 1] & (HALF - 1))
            pieces = []
            for ref in (high_s, low_s):
                for v in range(VARS):
                    pieces.append(jnp.where(here, ref[v * SLOTS + c : v * SLOTS + c + 1], 0.0).astype(BF16))
            parts.append(jnp.concatenate(pieces, axis=0))
        left = jnp.concatenate(parts, axis=1)
        total = contract(left, place_ref[:, first * LANES : (first + BATCH) * LANES])
        if first == 0:
            total_s[...] = total
        else:
            total_s[...] += total
    size = VARS * HALF
    for v in range(VARS):
        added = total_s[v * HALF : (v + 1) * HALF] + total_s[size + v * HALF : size + (v + 1) * HALF]
        out_ref[v] = turned(added)


def apply_block(wide_ref, k, which, xs):
    out = []
    for i in range(VARS):
        at = which * SQUARE + i * VARS
        total = wide_ref[k, at : at + 1] * xs[0]
        for j in range(1, VARS):
            total = total + wide_ref[k, at + j : at + j + 1] * xs[j]
        out.append(total)
    return out


def factor_at(factor_ref, which, k, first):
    return factor_ref[which * BLK + k, first : first + SPAN]


def solve_kernel(full, *refs):
    rows = FULL if full else BARE
    got_ref, point_ref, place_ref, wide_ref, factor_ref, order_ref, count_ref, state_ref, visc_hbm, forcing_hbm = refs[:10]
    refs = refs[10:]
    if full:
        maps_ref, refs = refs[0], refs[1:]
    chunk_ref, z_ref, resid_s, high_s, low_s, total_s, visc_s, forcing_s, sems = refs
    copies = fetch(((visc_hbm, visc_s), (forcing_hbm, forcing_s)), sems)
    order = order_of(order_ref)
    scatter(got_ref, point_ref, place_ref, resid_s, high_s, low_s, total_s)
    for copy in copies:
        copy.wait()
    residual(state_ref, forcing_s, visc_s, count_ref, resid_s)
    if full:
        for r in range(FULL - BARE):
            chunk_ref[pl.ds(BARE + r, TILES, stride=rows), :] = maps_ref[r]
    for first in range(0, TILES, SPAN):

        def put(r, value):
            chunk_ref[pl.ds(first * rows + r, SPAN, stride=rows), :] = value

        z = None
        for k in range(BLK):
            places = pl.ds(order[k] + BLK * first, SPAN, stride=BLK)
            scale = factor_at(factor_ref, DIAG, k, first)
            solved = [scale * x for x in apply_block(wide_ref, k, INV, [resid_s[j, places, :] for j in range(VARS)])]
            if k > 0:
                fall = factor_at(factor_ref, DOWN, k, first)
                solved = [fall * m + x for m, x in zip(apply_block(wide_ref, k, LOW, z), solved)]
            z = solved
            for i in range(VARS):
                z_ref[k, i, first : first + SPAN] = z[i]
        for i in range(VARS):
            put(i, z[i])
        y = z
        for k in reversed(range(BLK - 1)):
            rise = factor_at(factor_ref, RISE, k, first)
            moved = apply_block(wide_ref, k, UP, y)
            y = [z_ref[k, i, first : first + SPAN] + rise * moved[i] for i in range(VARS)]
        for i in range(VARS):
            put(VARS + i, y[i])


MATS = 6


def columns(mats, cols_ref):
    lane = lax.broadcasted_iota(jnp.int32, mats.shape, 1)
    mats = jnp.where(lane < SQUARE, mats, 0.0)
    packed = mats.astype(BF16).astype(F32)
    rest = mats - packed
    for n in (1, 2):
        part = rest.astype(BF16).astype(F32)
        rest = rest - part
        packed = packed + pltpu.roll(part, n * SQUARE, 1)
    packed = packed.astype(BF16)
    row = lax.broadcasted_iota(jnp.int32, (LANES, LANES), 0)
    row = row - jnp.where(row >= SQUARE, SQUARE, 0) - jnp.where(row >= 2 * SQUARE, SQUARE, 0)
    row = row.astype(F32).astype(BF16)
    for m in range(MATS):
        copies = [
            jnp.where(row == jnp.asarray(m * VARS + j, BF16), jnp.ones((), BF16), jnp.zeros((), BF16)) for j in range(VARS)
        ]
        spread = jnp.dot(packed, jnp.concatenate(copies, axis=1), preferred_element_type=F32)
        cols_ref[:, m * VARS * LANES : (m + 1) * VARS * LANES] = spread


def chain_kernel(rows, in_ref, coef_ref, out_ref, value_s, mid_s, mats_s, cols_s):
    for half in range(2):
        lines = coef_ref[pl.ds(FULL - 2 + half, TILES, stride=FULL), :]
        for n in range(3):
            shifted = pltpu.roll(lines, LANES - n * SQUARE, 1) if n else lines
            mats_s[pl.ds(3 * half + n, TILES, stride=8), :] = shifted
        for i in range(VARS):
            to = value_s if half == 0 else mid_s
            to[pl.ds(i, TILES, stride=8), :] = in_ref[pl.ds(half * VARS + i, TILES, stride=rows), :]

    for i in (VARS, VARS + 1):
        mats_s[pl.ds(i, TILES, stride=8), :] = jnp.zeros((TILES, LANES), F32)
    columns(mats_s[...], cols_s)

    def apply(here, m, x):
        terms = []
        for j in range(VARS):
            at = (m * VARS + j) * LANES
            terms.append(cols_s[here, at : at + LANES] * x[j])
        return ((terms[0] + terms[1]) + (terms[2] + terms[3])) + (terms[4] + terms[5])

    def spread(x):
        return [jnp.broadcast_to(x[j : j + 1], (VARS, LANES)) for j in range(VARS)]

    def coef(s, r):
        return coef_ref[FULL * s + BARE + r : FULL * s + BARE + r + 1]

    down = jnp.zeros((VARS, LANES), F32)
    for s in range(TILES):
        here = slice(8 * s, 8 * s + VARS)
        parts = spread(down)
        mid = mid_s[here]
        for k in range(BLK):
            mid = mid + coef(s, 2 + k) * apply(here, 2 + k, parts)
        mid_s[here] = mid
        after = coef(s, 0) * apply(here, 0, parts) + value_s[here]
        value_s[here] = down
        down = after
    up = jnp.zeros((VARS, LANES), F32)
    for s in reversed(range(TILES)):
        here = slice(8 * s, 8 * s + VARS)
        after = coef(s, 1) * apply(here, 1, spread(up)) + mid_s[here]
        mid_s[here] = up
        up = after
    for i in range(VARS):
        out_ref[pl.ds(i, TILES, stride=BARE), :] = value_s[pl.ds(i, TILES, stride=8), :]
        out_ref[pl.ds(VARS + i, TILES, stride=BARE), :] = mid_s[pl.ds(i, TILES, stride=8), :]


def finish(back_ref, z_ref, state_ref, wide_ref, factor_ref, order_ref, new_ref, corr_ref, star_s):
    order = order_of(order_ref)
    for first in range(0, TILES, SPAN):
        here = slice(first, first + SPAN)
        enter = [back_ref[pl.ds(first * BARE + i, SPAN, stride=BARE), :] for i in range(VARS)]
        for k in range(BLK):
            fall = factor_at(factor_ref, DOWN, k, first)
            enter = [fall * m for m in apply_block(wide_ref, k, LOW, enter)]
            for i in range(VARS):
                star_s[k, i, here] = enter[i] + z_ref[k, i, here]
        corr = [back_ref[pl.ds(first * BARE + VARS + i, SPAN, stride=BARE), :] for i in range(VARS)]
        for k in reversed(range(BLK)):
            rise = factor_at(factor_ref, RISE, k, first)
            moved = apply_block(wide_ref, k, UP, corr)
            corr = [star_s[k, i, here] + rise * moved[i] for i in range(VARS)]
            places = pl.ds(order[k] + BLK * first, SPAN, stride=BLK)
            for i in range(VARS):
                if corr_ref is not None:
                    corr_ref[i, places, :] = corr[i]
                new_ref[i, places, :] = state_ref[i, places, :] + corr[i]


def middle_kernel(
    back_ref, z_ref, state_ref, wide_ref, factor_ref, order_ref, block_hbm, point_hbm, weight_hbm, new_ref, out_ref,
    star_s, block_s, point_s, weight_s, pick_s, high_s, low_s, acc_s, sems,
):
    copies = fetch(((block_hbm, block_s), (point_hbm, point_s), (weight_hbm, weight_s)), sems)
    finish(back_ref, z_ref, state_ref, wide_ref, factor_ref, order_ref, new_ref, None, star_s)
    windows(new_ref, high_s, low_s)
    for copy in copies:
        copy.wait()
    picks(block_s, point_s, pick_s)
    gather(pick_s, point_s, weight_s, out_ref, high_s, low_s, acc_s)


def shape(*dims, dtype=F32):
    return pltpu.VMEM(dims, dtype)


def call(kernel, name, outs, operands, scratch=(), outside=(), beside=False):
    spaces = [pltpu.HBM if n in outside else pltpu.VMEM for n in range(len(operands))]
    return pl.pallas_call(
        kernel,
        out_shape=outs,
        in_specs=[pl.BlockSpec(memory_space=space) for space in spaces],
        out_specs=[VMEM] * len(outs),
        scratch_shapes=list(scratch),
        compiler_params=PARAMS,
        cost_estimate=BESIDE if beside else None,
        name=name,
    )(*[pltpu.with_memory_space_constraint(x, pltpu.HBM) if n in outside else x for n, x in enumerate(operands)])


def exchange(x, axes, count):
    parts = x.reshape(count, 1, -1)
    return lax.all_to_all(parts, axes, split_axis=0, concat_axis=0, tiled=True).reshape(x.shape)


def per_device(
    state, forcing, viscosity, inverses, lower_jac, upper_jac, diag_scale, lower_coupling, upper_coupling,
    donor_block, donor_point, donor_weight, fringe_block, fringe_point, block_order,
):
    big = (VARS, ROWS, LANES)
    state, forcing = to_rows(state[0]), to_rows(forcing[0])
    visc, diag, lowc, upc = (field_rows(x[0]) for x in (viscosity, diag_scale, lower_coupling, upper_coupling))
    inv, low_jac, up_jac = (x[0].transpose(1, 0, 2) for x in (inverses, lower_jac, upper_jac))
    src_block, src_point, dst_block, dst_point = (x[0].T for x in (donor_block, donor_point, fringe_block, fringe_point))
    weight = donor_weight[0].transpose(1, 2, 0)
    sent = VARS * (HALF + TAIL)
    gather_scratch = [pltpu.VMEM((sent, 256), BF16), pltpu.VMEM((sent, 256), BF16), pltpu.VMEM((256, LANES), F32)]
    star_scratch = [pltpu.VMEM((BLK, VARS, TILES, LANES), F32)]
    chain_scratch = [pltpu.VMEM((TILES * 8, LANES), F32) for _ in range(3)]
    chain_scratch += [pltpu.VMEM((TILES * 8, MATS * VARS * LANES), F32)]
    dma = pltpu.SemaphoreType.DMA

    def alike(x):
        return pltpu.VMEM(x.shape, x.dtype)

    source = (src_block, src_point, weight)
    source_scratch = [alike(x) for x in source] + [pltpu.VMEM((256, SLOTS * LANES), BF16)] + gather_scratch
    solve_scratch = [
        pltpu.VMEM(big, F32),
        pltpu.VMEM((VARS * SLOTS, LANES), F32),
        pltpu.VMEM((VARS * SLOTS, LANES), F32),
        pltpu.VMEM((2 * VARS * HALF, 256), F32),
        alike(visc),
        alike(forcing),
        dma((2,)),
    ]
    interp, state = call(
        first_kernel,
        "first",
        [shape(256, LANES), shape(*big)],
        (src_block, src_point, state, weight),
        source_scratch + [dma((4,))],
        outside=range(4),
    )
    got = exchange(interp, ("sweep", "grp"), 128)
    place, count, wide, factors, maps, dst_point, block_order = call(
        base_kernel,
        "base",
        [
            shape(256, SLOTS * LANES, dtype=BF16),
            shape(ROWS, LANES),
            shape(BLK, 3 * SQUARE, LANES),
            shape(3 * BLK, TILES, LANES),
            shape(FULL - BARE, TILES, LANES),
            alike(dst_point),
            alike(block_order),
        ],
        (dst_block, dst_point, diag, lowc, upc, inv, low_jac, up_jac, block_order),
        [alike(x) for x in (dst_block, diag, lowc, upc, inv, low_jac, up_jac)]
        + [
            pltpu.VMEM((HALF, SLOTS * LANES), BF16),
            pltpu.VMEM((3, VARS, BLK, VARS), F32),
            pltpu.VMEM((3 * BLK, VARS, VARS), F32),
            pltpu.VMEM((3 * SQUARE * BLK, LANES), F32),
            pltpu.VMEM((8, LANES), F32),
            dma((9,)),
        ],
        outside=range(9),
        beside=True,
    )

    def solve(full, got, state):
        operands = (got, dst_point, place, wide, factors, block_order, count, state, visc, forcing)
        operands += (maps,) if full else ()
        rows = FULL if full else BARE
        outs = [shape(TILES * rows, LANES), shape(BLK, VARS, TILES, LANES)]
        return call(lambda *refs: solve_kernel(full, *refs), "solve", outs, operands, solve_scratch, outside=(8, 9))

    def chain(values, coefs):
        rows = values.shape[0] // TILES
        outs = [shape(TILES * BARE, LANES)]
        return call(lambda *refs: chain_kernel(rows, *refs), "chain", outs, (values, coefs), chain_scratch)[0]

    chunk, z = solve(True, got, state)
    coefs = exchange(chunk, "sweep", TILES)
    back = exchange(chain(coefs, coefs), "sweep", TILES)
    state, interp = call(
        middle_kernel,
        "middle",
        [shape(*big), shape(256, LANES)],
        (back, z, state, wide, factors, block_order) + source,
        star_scratch + source_scratch + [dma((3,))],
        outside=(6, 7, 8),
    )
    got = exchange(interp, ("sweep", "grp"), 128)
    chunk, z = solve(False, got, state)
    back = exchange(chain(exchange(chunk, "sweep", TILES), coefs), "sweep", TILES)
    state, correction = call(
        finish, "finish", [jax.ShapeDtypeStruct(big, F32)] * 2, (back, z, state, wide, factors, block_order), star_scratch
    )
    return from_rows(state)[None], from_rows(correction)[None]


def solution(mesh):
    blocks = P("grp", "sweep", None, None)
    field = P("grp", "sweep", None)
    table = P(("sweep", "grp"), None, None)
    return jax.shard_map(
        per_device,
        mesh=mesh,
        in_specs=(
            blocks, blocks, field, blocks, blocks, blocks, field, field, field,
            table, table, P(("sweep", "grp"), None, None, None), table, table, P("grp", "sweep"),
        ),
        out_specs=(blocks, blocks),
        check_vma=False,
    )
```

```python
import jax
import jax.numpy as jnp
from jax import lax
from jax.experimental import pallas as pl
from jax.experimental.pallas import tpu as pltpu
from jax.sharding import PartitionSpec as P

F32 = jnp.float32
BF16 = jnp.bfloat16
VARS = 6
BLK = 4
TILES = 32
SLOTS = 32
LANES = 128
ROWS = TILES * BLK
HALF = 64
TAIL = 8
GROUP = 4
BATCH = 8
SPAN = 16
SQUARE = VARS * VARS
INV, LOW, UP = 0, 1, 2
DIAG, DOWN, RISE = 0, 1, 2
FULL = 20
BARE = 12
VMEM = pl.BlockSpec(memory_space=pltpu.VMEM)
PARAMS = pltpu.CompilerParams(vmem_limit_bytes=24 * 1024 * 1024)
BESIDE = pl.CostEstimate(flops=20_000_000_000, bytes_accessed=4_000_000, transcendentals=0)


def to_rows(x):
    return x.reshape(BLK, VARS, TILES, LANES).transpose(1, 2, 0, 3).reshape(VARS, ROWS, LANES)


def from_rows(x):
    return x.reshape(VARS, TILES, BLK, LANES).transpose(2, 0, 1, 3).reshape(BLK, VARS, TILES * LANES)


def field_rows(x):
    return x.reshape(BLK, TILES, LANES).transpose(1, 0, 2).reshape(ROWS, LANES)


def one_hot(count, index):
    size = (count, index.shape[1])
    places = lax.broadcasted_iota(jnp.int32, size, 0).astype(F32).astype(BF16)
    index = jnp.broadcast_to(index.astype(F32), size).astype(BF16)
    return jnp.where(places == index, jnp.ones((), BF16), jnp.zeros((), BF16))


def window_of(block, point):
    return ((point >> 6) & 1) * LANES + (point >> 7) * BLK + block


def split(x):
    high = x.astype(BF16)
    return high, (x - high.astype(F32)).astype(BF16)


def order_of(order_ref):
    order = order_ref[...]
    return [order[0, k] for k in range(BLK)]


def windows(state_ref, high_ref, low_ref):
    tails = []
    for v in range(VARS):
        turned = state_ref[v].T
        high, low = split(jnp.concatenate([turned[:HALF], turned[HALF:]], axis=1))
        high_ref[v * HALF : (v + 1) * HALF] = high
        low_ref[v * HALF : (v + 1) * HALF] = low
        following = pltpu.roll(turned[:TAIL], LANES - BLK, 1)
        tails.append(jnp.concatenate([turned[HALF : HALF + TAIL], following], axis=1))
    high, low = split(jnp.concatenate(tails, axis=0))
    high_ref[VARS * HALF :] = high
    low_ref[VARS * HALF :] = low


def stencil_of(point, weight_ref, c):
    ahead = lax.broadcasted_iota(jnp.int32, (HALF + TAIL, LANES), 0) - (point & (HALF - 1))
    row = jnp.zeros((HALF + TAIL, LANES), F32)
    for j in range(4):
        row = jnp.where(ahead == j, weight_ref[c, j : j + 1], row)
    return row


def picks(block_ref, point_ref, pick_ref):
    for c in range(SLOTS):
        window = window_of(block_ref[c : c + 1], point_ref[c : c + 1])
        pick_ref[:, c * LANES : (c + 1) * LANES] = one_hot(256, window)


def gather(pick_ref, point_ref, weight_ref, out_ref, high_ref, low_ref, acc_ref):
    acc_ref[VARS * SLOTS :] = jnp.zeros((256 - VARS * SLOTS, LANES), F32)
    for first in range(0, SLOTS, GROUP):
        pick = pick_ref[:, first * LANES : (first + GROUP) * LANES]
        found = jnp.dot(high_ref[...], pick, preferred_element_type=F32)
        found = found + jnp.dot(low_ref[...], pick, preferred_element_type=F32)
        for n in range(GROUP):
            cols = slice(n * LANES, (n + 1) * LANES)
            row = stencil_of(point_ref[first + n : first + n + 1], weight_ref, first + n)
            for v in range(VARS):
                main = found[v * HALF : (v + 1) * HALF, cols] * row[:HALF]
                start = VARS * HALF + v * TAIL
                tail = found[start : start + TAIL, cols] * row[HALF:]
                total = jnp.sum(main, axis=0, keepdims=True) + jnp.sum(tail, axis=0, keepdims=True)
                acc_ref[v * SLOTS + first + n : v * SLOTS + first + n + 1] = total
    out_ref[pl.ds(0, LANES, stride=2), :] = acc_ref[:LANES].T
    out_ref[pl.ds(1, LANES, stride=2), :] = acc_ref[LANES:].T


def fetch(pairs, sems):
    copies = [pltpu.make_async_copy(src, dst, sems.at[n]) for n, (src, dst) in enumerate(pairs)]
    for copy in copies:
        copy.start()
    return copies


def first_kernel(
    block_hbm, point_hbm, state_hbm, weight_hbm, out_ref, state_ref,
    block_s, point_s, weight_s, pick_s, high_s, low_s, acc_s, sems,
):
    pairs = ((block_hbm, block_s), (point_hbm, point_s), (state_hbm, state_ref), (weight_hbm, weight_s))
    copies = fetch(pairs, sems)
    copies[0].wait()
    copies[1].wait()
    picks(block_s, point_s, pick_s)
    copies[2].wait()
    windows(state_ref, high_s, low_s)
    copies[3].wait()
    gather(pick_s, point_s, weight_s, out_ref, high_s, low_s, acc_s)


def product(a, b):
    total = a[:, 0:1] * b[0:1, :]
    for j in range(1, VARS):
        total = total + a[:, j : j + 1] * b[j : j + 1, :]
    return total


def matrices(inv_ref, low_jac_ref, up_jac_ref, order, wide_ref, maps_ref, native_s, square_s, spread_s, mats_s):
    for i in range(VARS):
        row = inv_ref[i]
        native_s[INV, i] = row
        for which, jac_ref in ((LOW, low_jac_ref), (UP, up_jac_ref)):
            total = row[:, 0:1] * jac_ref[0]
            for j in range(1, VARS):
                total = total + row[:, j : j + 1] * jac_ref[j]
            native_s[which, i] = total
    for which in (INV, LOW, UP):
        for i in range(VARS):
            row = native_s[which, i]
            for j in range(VARS):
                at = ((which * VARS + i) * VARS + j) * BLK
                spread_s[at : at + BLK] = jnp.broadcast_to(row[:, j : j + 1], (BLK, LANES))
    for k in range(BLK):
        wide_ref[k] = spread_s[pl.ds(order[k], 3 * SQUARE, stride=BLK), :]
        for which in (LOW, UP):
            for i in range(VARS):
                square_s[which * BLK + k, i : i + 1, :] = native_s[which, i, pl.ds(order[k], 1), :]
    low = [square_s[LOW * BLK + k] for k in range(BLK)]
    up = [square_s[UP * BLK + k] for k in range(BLK)]
    downs, ups = [low[0]], [up[0]]
    for k in range(1, BLK):
        downs.append(product(low[k], downs[-1]))
        ups.append(product(ups[-1], up[k]))
    mixed = [downs[0]] + [product(ups[k - 1], downs[k]) for k in range(1, BLK)]
    mats_s[...] = jnp.zeros_like(mats_s)
    for m, mat in enumerate([downs[-1], ups[-1]] + mixed):
        mats_s[0:VARS, m * VARS : (m + 1) * VARS] = mat
    mats = mats_s[...]
    for half in range(2):
        line = mats[3 * half : 3 * half + 1]
        for n in (1, 2):
            line = line + pltpu.roll(mats[3 * half + n : 3 * half + n + 1], n * SQUARE, 1)
        maps_ref[6 + half] = jnp.broadcast_to(line, (TILES, LANES))


def residual(state_ref, forcing_ref, visc_ref, count_ref, out_ref):
    count = count_ref[...]
    lane = lax.broadcasted_iota(jnp.int32, (ROWS, LANES), 1)
    row = lax.broadcasted_iota(jnp.int32, (ROWS, LANES), 0)
    for v in range(VARS):
        x = state_ref[v]
        after = pltpu.roll(x, LANES - 1, 1)
        after = jnp.where(lane == LANES - 1, pltpu.roll(after, ROWS - BLK, 0), after)
        after = jnp.where((lane == LANES - 1) & (row >= ROWS - BLK), 0.0, after)
        before = pltpu.roll(x, 1, 1)
        before = jnp.where(lane == 0, pltpu.roll(before, BLK, 0), before)
        before = jnp.where((lane == 0) & (row < BLK), 0.0, before)
        out_ref[v] = forcing_ref[v] + visc_ref[...] * (after - 2.0 * x + before) + (out_ref[v] - count * x)


def turned(x):
    return jnp.concatenate([x[:, :LANES], x[:, LANES:]], axis=0).T


def contract(left, right):
    return lax.dot_general(left, right, (((1,), (1,)), ((), ())), preferred_element_type=F32)


def base_kernel(
    block_hbm, point_hbm, diag_hbm, lowc_hbm, upc_hbm, inv_hbm, low_jac_hbm, up_jac_hbm, order_hbm,
    place_ref, count_ref, wide_ref, factor_ref, maps_ref, point_ref, order_ref,
    block_ref, diag_ref, lowc_ref, upc_ref, inv_ref, low_jac_ref, up_jac_ref,
    left_s, native_s, square_s, spread_s, mats_s, sems,
):
    pairs = (
        (block_hbm, block_ref), (point_hbm, point_ref), (order_hbm, order_ref), (inv_hbm, inv_ref),
        (low_jac_hbm, low_jac_ref), (up_jac_hbm, up_jac_ref), (diag_hbm, diag_ref), (lowc_hbm, lowc_ref),
        (upc_hbm, upc_ref),
    )
    for copy in fetch(pairs, sems):
        copy.wait()
    order = order_of(order_ref)
    for c in range(SLOTS):
        cols = slice(c * LANES, (c + 1) * LANES)
        point = point_ref[c : c + 1]
        place_ref[:, cols] = one_hot(256, window_of(block_ref[c : c + 1], point))
        left_s[:, cols] = one_hot(HALF, point & (HALF - 1))
    matrices(inv_ref, low_jac_ref, up_jac_ref, order, wide_ref, maps_ref, native_s, square_s, spread_s, mats_s)
    down = up = None
    for k in range(BLK):
        rows = pl.ds(order[k], TILES, stride=BLK)
        scale = diag_ref[rows, :]
        fall, rise = scale * lowc_ref[rows, :], upc_ref[rows, :]
        factor_ref[DIAG * BLK + k] = scale
        factor_ref[DOWN * BLK + k] = fall
        factor_ref[RISE * BLK + k] = rise
        down = fall if k == 0 else down * fall
        maps_ref[2 + k] = down if k == 0 else down * up
        up = rise if k == 0 else up * rise
    maps_ref[0] = down
    maps_ref[1] = up
    count_ref[...] = turned(contract(left_s[...], place_ref[...]))


def scatter(got_ref, point_ref, place_ref, out_ref, high_s, low_s, total_s):
    high_s[:LANES] = got_ref[pl.ds(0, LANES, stride=2), :].T
    high_s[LANES:] = got_ref[pl.ds(1, LANES, stride=2), :].T[: VARS * SLOTS - LANES]
    got = high_s[...]
    high = got.astype(BF16).astype(F32)
    high_s[...] = high
    low_s[...] = got - high
    for first in range(0, SLOTS, BATCH):
        parts = []
        for c in range(first, first + BATCH):
            here = lax.broadcasted_iota(jnp.int32, (HALF, LANES), 0) == (point_ref[c : c + 1] & (HALF - 1))
            pieces = []
            for ref in (high_s, low_s):
                for v in range(VARS):
                    pieces.append(jnp.where(here, ref[v * SLOTS + c : v * SLOTS + c + 1], 0.0).astype(BF16))
            parts.append(jnp.concatenate(pieces, axis=0))
        left = jnp.concatenate(parts, axis=1)
        total = contract(left, place_ref[:, first * LANES : (first + BATCH) * LANES])
        if first == 0:
            total_s[...] = total
        else:
            total_s[...] += total
    size = VARS * HALF
    for v in range(VARS):
        added = total_s[v * HALF : (v + 1) * HALF] + total_s[size + v * HALF : size + (v + 1) * HALF]
        out_ref[v] = turned(added)


def apply_block(wide_ref, k, which, xs):
    out = []
    for i in range(VARS):
        at = which * SQUARE + i * VARS
        total = wide_ref[k, at : at + 1] * xs[0]
        for j in range(1, VARS):
            total = total + wide_ref[k, at + j : at + j + 1] * xs[j]
        out.append(total)
    return out


def factor_at(factor_ref, which, k, first):
    return factor_ref[which * BLK + k, first : first + SPAN]


def solve_kernel(full, *refs):
    rows = FULL if full else BARE
    got_ref, point_ref, place_ref, wide_ref, factor_ref, order_ref, count_ref, state_ref, visc_hbm, forcing_hbm = refs[:10]
    refs = refs[10:]
    if full:
        maps_ref, refs = refs[0], refs[1:]
    chunk_ref, z_ref, resid_s, high_s, low_s, total_s, visc_s, forcing_s, sems = refs
    copies = fetch(((visc_hbm, visc_s), (forcing_hbm, forcing_s)), sems)
    order = order_of(order_ref)
    scatter(got_ref, point_ref, place_ref, resid_s, high_s, low_s, total_s)
    for copy in copies:
        copy.wait()
    residual(state_ref, forcing_s, visc_s, count_ref, resid_s)
    if full:
        for r in range(FULL - BARE):
            chunk_ref[pl.ds(BARE + r, TILES, stride=rows), :] = maps_ref[r]
    for first in range(0, TILES, SPAN):

        def put(r, value):
            chunk_ref[pl.ds(first * rows + r, SPAN, stride=rows), :] = value

        z = None
        for k in range(BLK):
            places = pl.ds(order[k] + BLK * first, SPAN, stride=BLK)
            scale = factor_at(factor_ref, DIAG, k, first)
            solved = [scale * x for x in apply_block(wide_ref, k, INV, [resid_s[j, places, :] for j in range(VARS)])]
            if k > 0:
                fall = factor_at(factor_ref, DOWN, k, first)
                solved = [fall * m + x for m, x in zip(apply_block(wide_ref, k, LOW, z), solved)]
            z = solved
            for i in range(VARS):
                z_ref[k, i, first : first + SPAN] = z[i]
        for i in range(VARS):
            put(i, z[i])
        y = z
        for k in reversed(range(BLK - 1)):
            rise = factor_at(factor_ref, RISE, k, first)
            moved = apply_block(wide_ref, k, UP, y)
            y = [z_ref[k, i, first : first + SPAN] + rise * moved[i] for i in range(VARS)]
        for i in range(VARS):
            put(VARS + i, y[i])


MATS = 6


def columns(mats, cols_ref):
    lane = lax.broadcasted_iota(jnp.int32, mats.shape, 1)
    mats = jnp.where(lane < SQUARE, mats, 0.0)
    packed = mats.astype(BF16).astype(F32)
    rest = mats - packed
    for n in (1, 2):
        part = rest.astype(BF16).astype(F32)
        rest = rest - part
        packed = packed + pltpu.roll(part, n * SQUARE, 1)
    packed = packed.astype(BF16)
    row = lax.broadcasted_iota(jnp.int32, (LANES, LANES), 0)
    row = row - jnp.where(row >= SQUARE, SQUARE, 0) - jnp.where(row >= 2 * SQUARE, SQUARE, 0)
    row = row.astype(F32).astype(BF16)
    for m in range(MATS):
        copies = [
            jnp.where(row == jnp.asarray(m * VARS + j, BF16), jnp.ones((), BF16), jnp.zeros((), BF16)) for j in range(VARS)
        ]
        spread = jnp.dot(packed, jnp.concatenate(copies, axis=1), preferred_element_type=F32)
        cols_ref[:, m * VARS * LANES : (m + 1) * VARS * LANES] = spread


def first_chain_kernel(coef_ref, out_ref, cols_ref, value_s, mid_s, mats_s):
    for half in range(2):
        lines = coef_ref[pl.ds(FULL - 2 + half, TILES, stride=FULL), :]
        for n in range(3):
            shifted = pltpu.roll(lines, LANES - n * SQUARE, 1) if n else lines
            mats_s[pl.ds(3 * half + n, TILES, stride=8), :] = shifted
    for i in (VARS, VARS + 1):
        mats_s[pl.ds(i, TILES, stride=8), :] = jnp.zeros((TILES, LANES), F32)
    columns(mats_s[...], cols_ref)
    chain(FULL, coef_ref, coef_ref, cols_ref, out_ref, value_s, mid_s)


def second_chain_kernel(in_ref, coef_ref, cols_ref, out_ref, value_s, mid_s):
    chain(BARE, in_ref, coef_ref, cols_ref, out_ref, value_s, mid_s)


def chain(rows, in_ref, coef_ref, cols_ref, out_ref, value_s, mid_s):
    for i in range(VARS):
        value_s[pl.ds(i, TILES, stride=8), :] = in_ref[pl.ds(i, TILES, stride=rows), :]
        mid_s[pl.ds(i, TILES, stride=8), :] = in_ref[pl.ds(VARS + i, TILES, stride=rows), :]

    def apply(here, m, x):
        terms = []
        for j in range(VARS):
            at = (m * VARS + j) * LANES
            terms.append(cols_ref[here, at : at + LANES] * x[j])
        return ((terms[0] + terms[1]) + (terms[2] + terms[3])) + (terms[4] + terms[5])

    def spread(x):
        return [jnp.broadcast_to(x[j : j + 1], (VARS, LANES)) for j in range(VARS)]

    def coef(s, r):
        return coef_ref[FULL * s + BARE + r : FULL * s + BARE + r + 1]

    down = jnp.zeros((VARS, LANES), F32)
    for s in range(TILES):
        here = slice(8 * s, 8 * s + VARS)
        parts = spread(down)
        mid = mid_s[here]
        for k in range(BLK):
            mid = mid + coef(s, 2 + k) * apply(here, 2 + k, parts)
        mid_s[here] = mid
        after = coef(s, 0) * apply(here, 0, parts) + value_s[here]
        value_s[here] = down
        down = after
    up = jnp.zeros((VARS, LANES), F32)
    for s in reversed(range(TILES)):
        here = slice(8 * s, 8 * s + VARS)
        after = coef(s, 1) * apply(here, 1, spread(up)) + mid_s[here]
        mid_s[here] = up
        up = after
    for i in range(VARS):
        out_ref[pl.ds(i, TILES, stride=BARE), :] = value_s[pl.ds(i, TILES, stride=8), :]
        out_ref[pl.ds(VARS + i, TILES, stride=BARE), :] = mid_s[pl.ds(i, TILES, stride=8), :]


def finish(back_ref, z_ref, state_ref, wide_ref, factor_ref, order_ref, new_ref, corr_ref, star_s):
    order = order_of(order_ref)
    for first in range(0, TILES, SPAN):
        here = slice(first, first + SPAN)
        enter = [back_ref[pl.ds(first * BARE + i, SPAN, stride=BARE), :] for i in range(VARS)]
        for k in range(BLK):
            fall = factor_at(factor_ref, DOWN, k, first)
            enter = [fall * m for m in apply_block(wide_ref, k, LOW, enter)]
            for i in range(VARS):
                star_s[k, i, here] = enter[i] + z_ref[k, i, here]
        corr = [back_ref[pl.ds(first * BARE + VARS + i, SPAN, stride=BARE), :] for i in range(VARS)]
        for k in reversed(range(BLK)):
            rise = factor_at(factor_ref, RISE, k, first)
            moved = apply_block(wide_ref, k, UP, corr)
            corr = [star_s[k, i, here] + rise * moved[i] for i in range(VARS)]
            places = pl.ds(order[k] + BLK * first, SPAN, stride=BLK)
            for i in range(VARS):
                if corr_ref is not None:
                    corr_ref[i, places, :] = corr[i]
                new_ref[i, places, :] = state_ref[i, places, :] + corr[i]


def middle_kernel(
    back_ref, z_ref, state_ref, wide_ref, factor_ref, order_ref, block_hbm, point_hbm, weight_hbm, new_ref, out_ref,
    star_s, block_s, point_s, weight_s, pick_s, high_s, low_s, acc_s, sems,
):
    copies = fetch(((block_hbm, block_s), (point_hbm, point_s), (weight_hbm, weight_s)), sems)
    finish(back_ref, z_ref, state_ref, wide_ref, factor_ref, order_ref, new_ref, None, star_s)
    windows(new_ref, high_s, low_s)
    for copy in copies:
        copy.wait()
    picks(block_s, point_s, pick_s)
    gather(pick_s, point_s, weight_s, out_ref, high_s, low_s, acc_s)


def shape(*dims, dtype=F32):
    return pltpu.VMEM(dims, dtype)


def call(kernel, name, outs, operands, scratch=(), outside=(), beside=False):
    spaces = [pltpu.HBM if n in outside else pltpu.VMEM for n in range(len(operands))]
    return pl.pallas_call(
        kernel,
        out_shape=outs,
        in_specs=[pl.BlockSpec(memory_space=space) for space in spaces],
        out_specs=[VMEM] * len(outs),
        scratch_shapes=list(scratch),
        compiler_params=PARAMS,
        cost_estimate=BESIDE if beside else None,
        name=name,
    )(*[pltpu.with_memory_space_constraint(x, pltpu.HBM) if n in outside else x for n, x in enumerate(operands)])


def exchange(x, axes, count):
    parts = x.reshape(count, 1, -1)
    return lax.all_to_all(parts, axes, split_axis=0, concat_axis=0, tiled=True).reshape(x.shape)


def per_device(
    state, forcing, viscosity, inverses, lower_jac, upper_jac, diag_scale, lower_coupling, upper_coupling,
    donor_block, donor_point, donor_weight, fringe_block, fringe_point, block_order,
):
    big = (VARS, ROWS, LANES)
    state, forcing = to_rows(state[0]), to_rows(forcing[0])
    visc, diag, lowc, upc = (field_rows(x[0]) for x in (viscosity, diag_scale, lower_coupling, upper_coupling))
    inv, low_jac, up_jac = (x[0].transpose(1, 0, 2) for x in (inverses, lower_jac, upper_jac))
    src_block, src_point, dst_block, dst_point = (x[0].T for x in (donor_block, donor_point, fringe_block, fringe_point))
    weight = donor_weight[0].transpose(1, 2, 0)
    sent = VARS * (HALF + TAIL)
    gather_scratch = [pltpu.VMEM((sent, 256), BF16), pltpu.VMEM((sent, 256), BF16), pltpu.VMEM((256, LANES), F32)]
    star_scratch = [pltpu.VMEM((BLK, VARS, TILES, LANES), F32)]
    chain_scratch = [pltpu.VMEM((TILES * 8, LANES), F32) for _ in range(3)]
    dma = pltpu.SemaphoreType.DMA

    def alike(x):
        return pltpu.VMEM(x.shape, x.dtype)

    source = (src_block, src_point, weight)
    source_scratch = [alike(x) for x in source] + [pltpu.VMEM((256, SLOTS * LANES), BF16)] + gather_scratch
    solve_scratch = [
        pltpu.VMEM(big, F32),
        pltpu.VMEM((VARS * SLOTS, LANES), F32),
        pltpu.VMEM((VARS * SLOTS, LANES), F32),
        pltpu.VMEM((2 * VARS * HALF, 256), F32),
        alike(visc),
        alike(forcing),
        dma((2,)),
    ]
    interp, state = call(
        first_kernel,
        "first",
        [shape(256, LANES), shape(*big)],
        (src_block, src_point, state, weight),
        source_scratch + [dma((4,))],
        outside=range(4),
    )
    got = exchange(interp, ("sweep", "grp"), 128)
    place, count, wide, factors, maps, dst_point, block_order = call(
        base_kernel,
        "base",
        [
            shape(256, SLOTS * LANES, dtype=BF16),
            shape(ROWS, LANES),
            shape(BLK, 3 * SQUARE, LANES),
            shape(3 * BLK, TILES, LANES),
            shape(FULL - BARE, TILES, LANES),
            alike(dst_point),
            alike(block_order),
        ],
        (dst_block, dst_point, diag, lowc, upc, inv, low_jac, up_jac, block_order),
        [alike(x) for x in (dst_block, diag, lowc, upc, inv, low_jac, up_jac)]
        + [
            pltpu.VMEM((HALF, SLOTS * LANES), BF16),
            pltpu.VMEM((3, VARS, BLK, VARS), F32),
            pltpu.VMEM((3 * BLK, VARS, VARS), F32),
            pltpu.VMEM((3 * SQUARE * BLK, LANES), F32),
            pltpu.VMEM((8, LANES), F32),
            dma((9,)),
        ],
        outside=range(9),
        beside=True,
    )

    def solve(full, got, state):
        operands = (got, dst_point, place, wide, factors, block_order, count, state, visc, forcing)
        operands += (maps,) if full else ()
        rows = FULL if full else BARE
        outs = [shape(TILES * rows, LANES), shape(BLK, VARS, TILES, LANES)]
        return call(lambda *refs: solve_kernel(full, *refs), "solve", outs, operands, solve_scratch, outside=(8, 9))

    chunk, z = solve(True, got, state)
    coefs = exchange(chunk, "sweep", TILES)
    entering, cols = call(
        first_chain_kernel,
        "chain",
        [shape(TILES * BARE, LANES), shape(TILES * 8, MATS * VARS * LANES)],
        (coefs,),
        chain_scratch,
    )
    back = exchange(entering, "sweep", TILES)
    state, interp = call(
        middle_kernel,
        "middle",
        [shape(*big), shape(256, LANES)],
        (back, z, state, wide, factors, block_order) + source,
        star_scratch + source_scratch + [dma((3,))],
        outside=(6, 7, 8),
    )
    got = exchange(interp, ("sweep", "grp"), 128)
    chunk, z = solve(False, got, state)
    values = exchange(chunk, "sweep", TILES)
    (entering,) = call(
        second_chain_kernel, "chain", [shape(TILES * BARE, LANES)], (values, coefs, cols), chain_scratch[:2]
    )
    back = exchange(entering, "sweep", TILES)
    state, correction = call(
        finish, "finish", [jax.ShapeDtypeStruct(big, F32)] * 2, (back, z, state, wide, factors, block_order), star_scratch
    )
    return from_rows(state)[None], from_rows(correction)[None]


def solution(mesh):
    blocks = P("grp", "sweep", None, None)
    field = P("grp", "sweep", None)
    table = P(("sweep", "grp"), None, None)
    return jax.shard_map(
        per_device,
        mesh=mesh,
        in_specs=(
            blocks, blocks, field, blocks, blocks, blocks, field, field, field,
            table, table, P(("sweep", "grp"), None, None, None), table, table, P("grp", "sweep"),
        ),
        out_specs=(blocks, blocks),
        check_vma=False,
    )
```

```python
import jax
import jax.numpy as jnp
from jax import lax
from jax.experimental import pallas as pl
from jax.experimental.pallas import tpu as pltpu
from jax.sharding import PartitionSpec as P

F32 = jnp.float32
BF16 = jnp.bfloat16
VARS = 6
BLK = 4
TILES = 32
SLOTS = 32
LANES = 128
ROWS = TILES * BLK
HALF = 64
TAIL = 8
GROUP = 4
BATCH = 8
SPAN = 16
SQUARE = VARS * VARS
INV, LOW, UP = 0, 1, 2
DIAG, DOWN, RISE = 0, 1, 2
FULL = 20
BARE = 12
PARAMS = pltpu.CompilerParams(vmem_limit_bytes=24 * 1024 * 1024)
BESIDE = pl.CostEstimate(flops=20_000_000_000, bytes_accessed=4_000_000, transcendentals=0)


def to_rows(x):
    return x.reshape(BLK, VARS, TILES, LANES).transpose(1, 2, 0, 3).reshape(VARS, ROWS, LANES)


def from_rows(x):
    return x.reshape(VARS, TILES, BLK, LANES).transpose(2, 0, 1, 3).reshape(BLK, VARS, TILES * LANES)


def field_rows(x):
    return x.reshape(BLK, TILES, LANES).transpose(1, 0, 2).reshape(ROWS, LANES)


def one_hot(count, index):
    size = (count, index.shape[1])
    places = lax.broadcasted_iota(jnp.int32, size, 0).astype(F32).astype(BF16)
    index = jnp.broadcast_to(index.astype(F32), size).astype(BF16)
    return jnp.where(places == index, jnp.ones((), BF16), jnp.zeros((), BF16))


def window_of(block, point):
    return ((point >> 6) & 1) * LANES + (point >> 7) * BLK + block


def split(x):
    high = x.astype(BF16)
    return high, (x - high.astype(F32)).astype(BF16)


def order_of(order_ref):
    order = order_ref[...]
    return [order[0, k] for k in range(BLK)]


def windows(state_ref, high_ref, low_ref):
    tails = []
    for v in range(VARS):
        turned = state_ref[v].T
        high, low = split(jnp.concatenate([turned[:HALF], turned[HALF:]], axis=1))
        high_ref[v * HALF : (v + 1) * HALF] = high
        low_ref[v * HALF : (v + 1) * HALF] = low
        following = pltpu.roll(turned[:TAIL], LANES - BLK, 1)
        tails.append(jnp.concatenate([turned[HALF : HALF + TAIL], following], axis=1))
    high, low = split(jnp.concatenate(tails, axis=0))
    high_ref[VARS * HALF :] = high
    low_ref[VARS * HALF :] = low


def stencil_of(point, weight_ref, c):
    ahead = lax.broadcasted_iota(jnp.int32, (HALF + TAIL, LANES), 0) - (point & (HALF - 1))
    row = jnp.zeros((HALF + TAIL, LANES), F32)
    for j in range(4):
        row = jnp.where(ahead == j, weight_ref[c, j : j + 1], row)
    return row


def picks(block_ref, point_ref, pick_ref):
    for c in range(SLOTS):
        window = window_of(block_ref[c : c + 1], point_ref[c : c + 1])
        pick_ref[:, c * LANES : (c + 1) * LANES] = one_hot(256, window)


def gather(pick_ref, point_ref, weight_ref, out_ref, high_ref, low_ref, acc_ref):
    acc_ref[VARS * SLOTS :] = jnp.zeros((256 - VARS * SLOTS, LANES), F32)
    for first in range(0, SLOTS, GROUP):
        pick = pick_ref[:, first * LANES : (first + GROUP) * LANES]
        found = jnp.dot(high_ref[...], pick, preferred_element_type=F32)
        found = found + jnp.dot(low_ref[...], pick, preferred_element_type=F32)
        for n in range(GROUP):
            cols = slice(n * LANES, (n + 1) * LANES)
            row = stencil_of(point_ref[first + n : first + n + 1], weight_ref, first + n)
            for v in range(VARS):
                main = found[v * HALF : (v + 1) * HALF, cols] * row[:HALF]
                start = VARS * HALF + v * TAIL
                tail = found[start : start + TAIL, cols] * row[HALF:]
                total = jnp.sum(main, axis=0, keepdims=True) + jnp.sum(tail, axis=0, keepdims=True)
                acc_ref[v * SLOTS + first + n : v * SLOTS + first + n + 1] = total
    out_ref[pl.ds(0, LANES, stride=2), :] = acc_ref[:LANES].T
    out_ref[pl.ds(1, LANES, stride=2), :] = acc_ref[LANES:].T


def fetch(pairs, sems):
    copies = [pltpu.make_async_copy(src, dst, sems.at[n]) for n, (src, dst) in enumerate(pairs)]
    for copy in copies:
        copy.start()
    return copies


def first_kernel(
    block_hbm, point_hbm, state_hbm, weight_hbm, out_ref, state_ref,
    block_s, point_s, weight_s, pick_s, high_s, low_s, acc_s, sems,
):
    pairs = ((block_hbm, block_s), (point_hbm, point_s), (state_hbm, state_ref), (weight_hbm, weight_s))
    copies = fetch(pairs, sems)
    copies[0].wait()
    copies[1].wait()
    picks(block_s, point_s, pick_s)
    copies[2].wait()
    windows(state_ref, high_s, low_s)
    copies[3].wait()
    gather(pick_s, point_s, weight_s, out_ref, high_s, low_s, acc_s)


def product(a, b):
    total = a[:, 0:1] * b[0:1, :]
    for j in range(1, VARS):
        total = total + a[:, j : j + 1] * b[j : j + 1, :]
    return total


def matrices(inv_ref, low_jac_ref, up_jac_ref, order, wide_ref, maps_ref, native_s, square_s, spread_s, mats_s):
    for i in range(VARS):
        row = inv_ref[i]
        native_s[INV, i] = row
        for which, jac_ref in ((LOW, low_jac_ref), (UP, up_jac_ref)):
            total = row[:, 0:1] * jac_ref[0]
            for j in range(1, VARS):
                total = total + row[:, j : j + 1] * jac_ref[j]
            native_s[which, i] = total
    for which in (INV, LOW, UP):
        for i in range(VARS):
            row = native_s[which, i]
            for j in range(VARS):
                at = ((which * VARS + i) * VARS + j) * BLK
                spread_s[at : at + BLK] = jnp.broadcast_to(row[:, j : j + 1], (BLK, LANES))
    for k in range(BLK):
        wide_ref[k] = spread_s[pl.ds(order[k], 3 * SQUARE, stride=BLK), :]
        for which in (LOW, UP):
            for i in range(VARS):
                square_s[which * BLK + k, i : i + 1, :] = native_s[which, i, pl.ds(order[k], 1), :]
    low = [square_s[LOW * BLK + k] for k in range(BLK)]
    up = [square_s[UP * BLK + k] for k in range(BLK)]
    downs, ups = [low[0]], [up[0]]
    for k in range(1, BLK):
        downs.append(product(low[k], downs[-1]))
        ups.append(product(ups[-1], up[k]))
    mixed = [downs[0]] + [product(ups[k - 1], downs[k]) for k in range(1, BLK)]
    mats_s[...] = jnp.zeros_like(mats_s)
    for m, mat in enumerate([downs[-1], ups[-1]] + mixed):
        mats_s[0:VARS, m * VARS : (m + 1) * VARS] = mat
    mats = mats_s[...]
    for half in range(2):
        line = mats[3 * half : 3 * half + 1]
        for n in (1, 2):
            line = line + pltpu.roll(mats[3 * half + n : 3 * half + n + 1], n * SQUARE, 1)
        maps_ref[6 + half] = jnp.broadcast_to(line, (TILES, LANES))


def residual(state_ref, forcing_ref, visc_ref, count_ref, out_ref):
    count = count_ref[...]
    lane = lax.broadcasted_iota(jnp.int32, (ROWS, LANES), 1)
    row = lax.broadcasted_iota(jnp.int32, (ROWS, LANES), 0)
    for v in range(VARS):
        x = state_ref[v]
        after = pltpu.roll(x, LANES - 1, 1)
        after = jnp.where(lane == LANES - 1, pltpu.roll(after, ROWS - BLK, 0), after)
        after = jnp.where((lane == LANES - 1) & (row >= ROWS - BLK), 0.0, after)
        before = pltpu.roll(x, 1, 1)
        before = jnp.where(lane == 0, pltpu.roll(before, BLK, 0), before)
        before = jnp.where((lane == 0) & (row < BLK), 0.0, before)
        out_ref[v] = forcing_ref[v] + visc_ref[...] * (after - 2.0 * x + before) + (out_ref[v] - count * x)


def turned(x):
    return jnp.concatenate([x[:, :LANES], x[:, LANES:]], axis=0).T


def contract(left, right):
    return lax.dot_general(left, right, (((1,), (1,)), ((), ())), preferred_element_type=F32)


def base_kernel(
    block_hbm, point_hbm, diag_hbm, lowc_hbm, upc_hbm, inv_hbm, low_jac_hbm, up_jac_hbm, order_hbm,
    place_ref, count_ref, wide_ref, factor_ref, maps_ref, point_ref, order_ref,
    block_ref, diag_ref, lowc_ref, upc_ref, inv_ref, low_jac_ref, up_jac_ref,
    left_s, native_s, square_s, spread_s, mats_s, sems,
):
    pairs = (
        (block_hbm, block_ref), (point_hbm, point_ref), (order_hbm, order_ref), (inv_hbm, inv_ref),
        (low_jac_hbm, low_jac_ref), (up_jac_hbm, up_jac_ref), (diag_hbm, diag_ref), (lowc_hbm, lowc_ref),
        (upc_hbm, upc_ref),
    )
    for copy in fetch(pairs, sems):
        copy.wait()
    order = order_of(order_ref)
    for c in range(SLOTS):
        cols = slice(c * LANES, (c + 1) * LANES)
        point = point_ref[c : c + 1]
        place_ref[:, cols] = one_hot(256, window_of(block_ref[c : c + 1], point))
        left_s[:, cols] = one_hot(HALF, point & (HALF - 1))
    matrices(inv_ref, low_jac_ref, up_jac_ref, order, wide_ref, maps_ref, native_s, square_s, spread_s, mats_s)
    down = up = None
    for k in range(BLK):
        rows = pl.ds(order[k], TILES, stride=BLK)
        scale = diag_ref[rows, :]
        fall, rise = scale * lowc_ref[rows, :], upc_ref[rows, :]
        factor_ref[DIAG * BLK + k] = scale
        factor_ref[DOWN * BLK + k] = fall
        factor_ref[RISE * BLK + k] = rise
        down = fall if k == 0 else down * fall
        maps_ref[2 + k] = down if k == 0 else down * up
        up = rise if k == 0 else up * rise
    maps_ref[0] = down
    maps_ref[1] = up
    count_ref[...] = turned(contract(left_s[...], place_ref[...]))


def scatter(got_ref, point_ref, place_ref, out_ref, high_s, low_s, total_s):
    high_s[:LANES] = got_ref[pl.ds(0, LANES, stride=2), :].T
    high_s[LANES:] = got_ref[pl.ds(1, LANES, stride=2), :].T[: VARS * SLOTS - LANES]
    got = high_s[...]
    high = got.astype(BF16).astype(F32)
    high_s[...] = high
    low_s[...] = got - high
    for first in range(0, SLOTS, BATCH):
        parts = []
        for c in range(first, first + BATCH):
            here = lax.broadcasted_iota(jnp.int32, (HALF, LANES), 0) == (point_ref[c : c + 1] & (HALF - 1))
            pieces = []
            for ref in (high_s, low_s):
                for v in range(VARS):
                    pieces.append(jnp.where(here, ref[v * SLOTS + c : v * SLOTS + c + 1], 0.0).astype(BF16))
            parts.append(jnp.concatenate(pieces, axis=0))
        left = jnp.concatenate(parts, axis=1)
        total = contract(left, place_ref[:, first * LANES : (first + BATCH) * LANES])
        if first == 0:
            total_s[...] = total
        else:
            total_s[...] += total
    size = VARS * HALF
    for v in range(VARS):
        added = total_s[v * HALF : (v + 1) * HALF] + total_s[size + v * HALF : size + (v + 1) * HALF]
        out_ref[v] = turned(added)


def apply_block(wide_ref, k, which, xs):
    out = []
    for i in range(VARS):
        at = which * SQUARE + i * VARS
        total = wide_ref[k, at : at + 1] * xs[0]
        for j in range(1, VARS):
            total = total + wide_ref[k, at + j : at + j + 1] * xs[j]
        out.append(total)
    return out


def factor_at(factor_ref, which, k, first):
    return factor_ref[which * BLK + k, first : first + SPAN]


def solve_kernel(full, *refs):
    rows = FULL if full else BARE
    got_ref, point_ref, place_ref, wide_ref, factor_ref, order_ref, count_ref, state_ref, visc_hbm, forcing_hbm = refs[:10]
    refs = refs[10:]
    if full:
        maps_ref, refs = refs[0], refs[1:]
    chunk_ref, z_ref, resid_s, high_s, low_s, total_s, visc_s, forcing_s, sems = refs
    copies = fetch(((visc_hbm, visc_s), (forcing_hbm, forcing_s)), sems)
    order = order_of(order_ref)
    if full:
        maps = maps_ref[...]
        for r in range(FULL - BARE):
            chunk_ref[pl.ds(BARE + r, TILES, stride=rows), :] = maps[r]
    scatter(got_ref, point_ref, place_ref, resid_s, high_s, low_s, total_s)
    for copy in copies:
        copy.wait()
    residual(state_ref, forcing_s, visc_s, count_ref, resid_s)
    for first in range(0, TILES, SPAN):

        def put(r, value):
            chunk_ref[pl.ds(first * rows + r, SPAN, stride=rows), :] = value

        z = None
        for k in range(BLK):
            places = pl.ds(order[k] + BLK * first, SPAN, stride=BLK)
            scale = factor_at(factor_ref, DIAG, k, first)
            solved = [scale * x for x in apply_block(wide_ref, k, INV, [resid_s[j, places, :] for j in range(VARS)])]
            if k > 0:
                fall = factor_at(factor_ref, DOWN, k, first)
                solved = [fall * m + x for m, x in zip(apply_block(wide_ref, k, LOW, z), solved)]
            z = solved
            for i in range(VARS):
                z_ref[k, i, first : first + SPAN] = z[i]
        for i in range(VARS):
            put(i, z[i])
        y = z
        for k in reversed(range(BLK - 1)):
            rise = factor_at(factor_ref, RISE, k, first)
            moved = apply_block(wide_ref, k, UP, y)
            y = [z_ref[k, i, first : first + SPAN] + rise * moved[i] for i in range(VARS)]
        for i in range(VARS):
            put(VARS + i, y[i])


MATS = 6


def columns(mats, cols_ref):
    lane = lax.broadcasted_iota(jnp.int32, mats.shape, 1)
    mats = jnp.where(lane < SQUARE, mats, 0.0)
    packed = mats.astype(BF16).astype(F32)
    rest = mats - packed
    for n in (1, 2):
        part = rest.astype(BF16).astype(F32)
        rest = rest - part
        packed = packed + pltpu.roll(part, n * SQUARE, 1)
    packed = packed.astype(BF16)
    row = lax.broadcasted_iota(jnp.int32, (LANES, LANES), 0)
    row = row - jnp.where(row >= SQUARE, SQUARE, 0) - jnp.where(row >= 2 * SQUARE, SQUARE, 0)
    row = row.astype(F32).astype(BF16)
    for m in range(MATS):
        copies = [
            jnp.where(row == jnp.asarray(m * VARS + j, BF16), jnp.ones((), BF16), jnp.zeros((), BF16)) for j in range(VARS)
        ]
        spread = jnp.dot(packed, jnp.concatenate(copies, axis=1), preferred_element_type=F32)
        cols_ref[:, m * VARS * LANES : (m + 1) * VARS * LANES] = spread


def first_chain_kernel(coef_ref, out_ref, cols_ref, value_s, mid_s, mats_s):
    for half in range(2):
        lines = coef_ref[pl.ds(FULL - 2 + half, TILES, stride=FULL), :]
        for n in range(3):
            shifted = pltpu.roll(lines, LANES - n * SQUARE, 1) if n else lines
            mats_s[pl.ds(3 * half + n, TILES, stride=8), :] = shifted
    for i in (VARS, VARS + 1):
        mats_s[pl.ds(i, TILES, stride=8), :] = jnp.zeros((TILES, LANES), F32)
    columns(mats_s[...], cols_ref)
    chain(FULL, coef_ref, coef_ref, cols_ref, out_ref, value_s, mid_s)


def second_chain_kernel(in_ref, coef_ref, cols_ref, out_ref, value_s, mid_s):
    chain(BARE, in_ref, coef_ref, cols_ref, out_ref, value_s, mid_s)


def chain(rows, in_ref, coef_ref, cols_ref, out_ref, value_s, mid_s):
    for i in range(VARS):
        value_s[pl.ds(i, TILES, stride=8), :] = in_ref[pl.ds(i, TILES, stride=rows), :]
        mid_s[pl.ds(i, TILES, stride=8), :] = in_ref[pl.ds(VARS + i, TILES, stride=rows), :]

    def apply(here, m, x):
        terms = []
        for j in range(VARS):
            at = (m * VARS + j) * LANES
            terms.append(cols_ref[here, at : at + LANES] * x[j])
        return ((terms[0] + terms[1]) + (terms[2] + terms[3])) + (terms[4] + terms[5])

    def spread(x):
        return [jnp.broadcast_to(x[j : j + 1], (VARS, LANES)) for j in range(VARS)]

    def coef(s, r):
        return coef_ref[FULL * s + BARE + r : FULL * s + BARE + r + 1]

    down = jnp.zeros((VARS, LANES), F32)
    for s in range(TILES):
        here = slice(8 * s, 8 * s + VARS)
        parts = spread(down)
        mid = mid_s[here]
        for k in range(BLK):
            mid = mid + coef(s, 2 + k) * apply(here, 2 + k, parts)
        mid_s[here] = mid
        after = coef(s, 0) * apply(here, 0, parts) + value_s[here]
        value_s[here] = down
        down = after
    up = jnp.zeros((VARS, LANES), F32)
    for s in reversed(range(TILES)):
        here = slice(8 * s, 8 * s + VARS)
        after = coef(s, 1) * apply(here, 1, spread(up)) + mid_s[here]
        mid_s[here] = up
        up = after
    for i in range(VARS):
        out_ref[pl.ds(i, TILES, stride=BARE), :] = value_s[pl.ds(i, TILES, stride=8), :]
        out_ref[pl.ds(VARS + i, TILES, stride=BARE), :] = mid_s[pl.ds(i, TILES, stride=8), :]


def finish(back_ref, z_ref, state_ref, wide_ref, factor_ref, order_ref, new_ref, corr_ref, star_s, ready=None):
    order = order_of(order_ref)
    for first in range(0, TILES, SPAN):
        here = slice(first, first + SPAN)
        enter = [back_ref[pl.ds(first * BARE + i, SPAN, stride=BARE), :] for i in range(VARS)]
        for k in range(BLK):
            fall = factor_at(factor_ref, DOWN, k, first)
            enter = [fall * m for m in apply_block(wide_ref, k, LOW, enter)]
            for i in range(VARS):
                star_s[k, i, here] = enter[i] + z_ref[k, i, here]
        corr = [back_ref[pl.ds(first * BARE + VARS + i, SPAN, stride=BARE), :] for i in range(VARS)]
        for k in reversed(range(BLK)):
            rise = factor_at(factor_ref, RISE, k, first)
            moved = apply_block(wide_ref, k, UP, corr)
            corr = [star_s[k, i, here] + rise * moved[i] for i in range(VARS)]
            places = pl.ds(order[k] + BLK * first, SPAN, stride=BLK)
            for i in range(VARS):
                if corr_ref is not None:
                    corr_ref[i, places, :] = corr[i]
                new_ref[i, places, :] = state_ref[i, places, :] + corr[i]
        if ready is not None:
            ready(first)


def last_kernel(
    back_ref, z_ref, state_ref, wide_ref, factor_ref, order_ref, new_hbm, corr_hbm, star_s, new_s, corr_s, sems
):
    copies = []

    def ready(first):
        rows = pl.ds(first * BLK, SPAN * BLK)
        for src, dst in ((new_s, new_hbm), (corr_s, corr_hbm)):
            copy = pltpu.make_async_copy(src.at[:, rows, :], dst.at[:, rows, :], sems.at[len(copies)])
            copy.start()
            copies.append(copy)

    finish(back_ref, z_ref, state_ref, wide_ref, factor_ref, order_ref, new_s, corr_s, star_s, ready)
    for copy in copies:
        copy.wait()


def middle_kernel(
    back_ref, z_ref, state_ref, wide_ref, factor_ref, order_ref, block_hbm, point_hbm, weight_hbm, new_ref, out_ref,
    star_s, block_s, point_s, weight_s, pick_s, high_s, low_s, acc_s, sems,
):
    copies = fetch(((block_hbm, block_s), (point_hbm, point_s), (weight_hbm, weight_s)), sems)
    finish(back_ref, z_ref, state_ref, wide_ref, factor_ref, order_ref, new_ref, None, star_s)
    windows(new_ref, high_s, low_s)
    for copy in copies:
        copy.wait()
    picks(block_s, point_s, pick_s)
    gather(pick_s, point_s, weight_s, out_ref, high_s, low_s, acc_s)


def shape(*dims, dtype=F32):
    return pltpu.VMEM(dims, dtype)


def call(kernel, name, outs, operands, scratch=(), outside=(), beside=False, out_space=pltpu.VMEM):
    spaces = [pltpu.HBM if n in outside else pltpu.VMEM for n in range(len(operands))]
    return pl.pallas_call(
        kernel,
        out_shape=outs,
        in_specs=[pl.BlockSpec(memory_space=space) for space in spaces],
        out_specs=[pl.BlockSpec(memory_space=out_space)] * len(outs),
        scratch_shapes=list(scratch),
        compiler_params=PARAMS,
        cost_estimate=BESIDE if beside else None,
        name=name,
    )(*[pltpu.with_memory_space_constraint(x, pltpu.HBM) if n in outside else x for n, x in enumerate(operands)])


def exchange(x, axes, count):
    parts = x.reshape(count, 1, -1)
    return lax.all_to_all(parts, axes, split_axis=0, concat_axis=0, tiled=True).reshape(x.shape)


def per_device(
    state, forcing, viscosity, inverses, lower_jac, upper_jac, diag_scale, lower_coupling, upper_coupling,
    donor_block, donor_point, donor_weight, fringe_block, fringe_point, block_order,
):
    big = (VARS, ROWS, LANES)
    state, forcing = to_rows(state[0]), to_rows(forcing[0])
    visc, diag, lowc, upc = (field_rows(x[0]) for x in (viscosity, diag_scale, lower_coupling, upper_coupling))
    inv, low_jac, up_jac = (x[0].transpose(1, 0, 2) for x in (inverses, lower_jac, upper_jac))
    src_block, src_point, dst_block, dst_point = (x[0].T for x in (donor_block, donor_point, fringe_block, fringe_point))
    weight = donor_weight[0].transpose(1, 2, 0)
    sent = VARS * (HALF + TAIL)
    gather_scratch = [pltpu.VMEM((sent, 256), BF16), pltpu.VMEM((sent, 256), BF16), pltpu.VMEM((256, LANES), F32)]
    star_scratch = [pltpu.VMEM((BLK, VARS, TILES, LANES), F32)]
    chain_scratch = [pltpu.VMEM((TILES * 8, LANES), F32) for _ in range(3)]
    dma = pltpu.SemaphoreType.DMA

    def alike(x):
        return pltpu.VMEM(x.shape, x.dtype)

    source = (src_block, src_point, weight)
    source_scratch = [alike(x) for x in source] + [pltpu.VMEM((256, SLOTS * LANES), BF16)] + gather_scratch
    solve_scratch = [
        pltpu.VMEM(big, F32),
        pltpu.VMEM((VARS * SLOTS, LANES), F32),
        pltpu.VMEM((VARS * SLOTS, LANES), F32),
        pltpu.VMEM((2 * VARS * HALF, 256), F32),
        alike(visc),
        alike(forcing),
        dma((2,)),
    ]
    interp, state = call(
        first_kernel,
        "first",
        [shape(256, LANES), shape(*big)],
        (src_block, src_point, state, weight),
        source_scratch + [dma((4,))],
        outside=range(4),
    )
    got = exchange(interp, ("sweep", "grp"), 128)
    place, count, wide, factors, maps, dst_point, block_order = call(
        base_kernel,
        "base",
        [
            shape(256, SLOTS * LANES, dtype=BF16),
            shape(ROWS, LANES),
            shape(BLK, 3 * SQUARE, LANES),
            shape(3 * BLK, TILES, LANES),
            shape(FULL - BARE, TILES, LANES),
            alike(dst_point),
            alike(block_order),
        ],
        (dst_block, dst_point, diag, lowc, upc, inv, low_jac, up_jac, block_order),
        [alike(x) for x in (dst_block, diag, lowc, upc, inv, low_jac, up_jac)]
        + [
            pltpu.VMEM((HALF, SLOTS * LANES), BF16),
            pltpu.VMEM((3, VARS, BLK, VARS), F32),
            pltpu.VMEM((3 * BLK, VARS, VARS), F32),
            pltpu.VMEM((3 * SQUARE * BLK, LANES), F32),
            pltpu.VMEM((8, LANES), F32),
            dma((9,)),
        ],
        outside=range(9),
        beside=True,
    )

    def solve(full, got, state):
        operands = (got, dst_point, place, wide, factors, block_order, count, state, visc, forcing)
        operands += (maps,) if full else ()
        rows = FULL if full else BARE
        outs = [shape(TILES * rows, LANES), shape(BLK, VARS, TILES, LANES)]
        return call(lambda *refs: solve_kernel(full, *refs), "solve", outs, operands, solve_scratch, outside=(8, 9))

    chunk, z = solve(True, got, state)
    coefs = exchange(chunk, "sweep", TILES)
    entering, cols = call(
        first_chain_kernel,
        "chain",
        [shape(TILES * BARE, LANES), shape(TILES * 8, MATS * VARS * LANES)],
        (coefs,),
        chain_scratch,
    )
    back = exchange(entering, "sweep", TILES)
    state, interp = call(
        middle_kernel,
        "middle",
        [shape(*big), shape(256, LANES)],
        (back, z, state, wide, factors, block_order) + source,
        star_scratch + source_scratch + [dma((3,))],
        outside=(6, 7, 8),
    )
    got = exchange(interp, ("sweep", "grp"), 128)
    chunk, z = solve(False, got, state)
    values = exchange(chunk, "sweep", TILES)
    (entering,) = call(
        second_chain_kernel, "chain", [shape(TILES * BARE, LANES)], (values, coefs, cols), chain_scratch[:2]
    )
    back = exchange(entering, "sweep", TILES)
    state, correction = call(
        last_kernel,
        "last",
        [jax.ShapeDtypeStruct(big, F32)] * 2,
        (back, z, state, wide, factors, block_order),
        star_scratch + [pltpu.VMEM(big, F32), pltpu.VMEM(big, F32), dma((2 * TILES // SPAN,))],
        out_space=pltpu.HBM,
    )
    return from_rows(state)[None], from_rows(correction)[None]


def solution(mesh):
    blocks = P("grp", "sweep", None, None)
    field = P("grp", "sweep", None)
    table = P(("sweep", "grp"), None, None)
    return jax.shard_map(
        per_device,
        mesh=mesh,
        in_specs=(
            blocks, blocks, field, blocks, blocks, blocks, field, field, field,
            table, table, P(("sweep", "grp"), None, None, None), table, table, P("grp", "sweep"),
        ),
        out_specs=(blocks, blocks),
        check_vma=False,
    )
```

```python
import jax
import jax.numpy as jnp
from jax import lax
from jax.experimental import pallas as pl
from jax.experimental.pallas import tpu as pltpu
from jax.sharding import PartitionSpec as P

F32 = jnp.float32
BF16 = jnp.bfloat16
VARS = 6
BLK = 4
TILES = 32
SLOTS = 32
LANES = 128
ROWS = TILES * BLK
HALF = 64
TAIL = 8
GROUP = 4
BATCH = 8
SPAN = 16
SQUARE = VARS * VARS
INV, LOW, UP = 0, 1, 2
DIAG, DOWN, RISE = 0, 1, 2
FULL = 20
BARE = 12
PARAMS = pltpu.CompilerParams(vmem_limit_bytes=24 * 1024 * 1024)
BESIDE = pl.CostEstimate(flops=20_000_000_000, bytes_accessed=4_000_000, transcendentals=0)


def to_rows(x):
    return x.reshape(BLK, VARS, TILES, LANES).transpose(1, 2, 0, 3).reshape(VARS, ROWS, LANES)


def from_rows(x):
    return x.reshape(VARS, TILES, BLK, LANES).transpose(2, 0, 1, 3).reshape(BLK, VARS, TILES * LANES)


def field_rows(x):
    return x.reshape(BLK, TILES, LANES).transpose(1, 0, 2).reshape(ROWS, LANES)


def one_hot(count, index):
    size = (count, index.shape[1])
    places = lax.broadcasted_iota(jnp.int32, size, 0).astype(F32).astype(BF16)
    index = jnp.broadcast_to(index.astype(F32), size).astype(BF16)
    return jnp.where(places == index, jnp.ones((), BF16), jnp.zeros((), BF16))


def window_of(block, point):
    return ((point >> 6) & 1) * LANES + (point >> 7) * BLK + block


def split(x):
    high = x.astype(BF16)
    return high, (x - high.astype(F32)).astype(BF16)


def order_of(order_ref):
    order = order_ref[...]
    return [order[0, k] for k in range(BLK)]


def windows(state_ref, high_ref, low_ref):
    tails = []
    for v in range(VARS):
        turned = state_ref[v].T
        high, low = split(jnp.concatenate([turned[:HALF], turned[HALF:]], axis=1))
        high_ref[v * HALF : (v + 1) * HALF] = high
        low_ref[v * HALF : (v + 1) * HALF] = low
        following = pltpu.roll(turned[:TAIL], LANES - BLK, 1)
        tails.append(jnp.concatenate([turned[HALF : HALF + TAIL], following], axis=1))
    high, low = split(jnp.concatenate(tails, axis=0))
    high_ref[VARS * HALF :] = high
    low_ref[VARS * HALF :] = low


def stencil_of(point, weight_ref, c):
    ahead = lax.broadcasted_iota(jnp.int32, (HALF + TAIL, LANES), 0) - (point & (HALF - 1))
    row = jnp.zeros((HALF + TAIL, LANES), F32)
    for j in range(4):
        row = jnp.where(ahead == j, weight_ref[c, j : j + 1], row)
    return row


def picks(block_ref, point_ref, pick_ref):
    for c in range(SLOTS):
        window = window_of(block_ref[c : c + 1], point_ref[c : c + 1])
        pick_ref[:, c * LANES : (c + 1) * LANES] = one_hot(256, window)


def gather(pick_ref, point_ref, weight_ref, out_ref, high_ref, low_ref, acc_ref):
    acc_ref[VARS * SLOTS :] = jnp.zeros((256 - VARS * SLOTS, LANES), F32)
    for first in range(0, SLOTS, GROUP):
        pick = pick_ref[:, first * LANES : (first + GROUP) * LANES]
        found = jnp.dot(high_ref[...], pick, preferred_element_type=F32)
        found = found + jnp.dot(low_ref[...], pick, preferred_element_type=F32)
        for n in range(GROUP):
            cols = slice(n * LANES, (n + 1) * LANES)
            row = stencil_of(point_ref[first + n : first + n + 1], weight_ref, first + n)
            for v in range(VARS):
                main = found[v * HALF : (v + 1) * HALF, cols] * row[:HALF]
                start = VARS * HALF + v * TAIL
                tail = found[start : start + TAIL, cols] * row[HALF:]
                total = jnp.sum(main, axis=0, keepdims=True) + jnp.sum(tail, axis=0, keepdims=True)
                acc_ref[v * SLOTS + first + n : v * SLOTS + first + n + 1] = total
    out_ref[pl.ds(0, LANES, stride=2), :] = acc_ref[:LANES].T
    out_ref[pl.ds(1, LANES, stride=2), :] = acc_ref[LANES:].T


def fetch(pairs, sems):
    copies = [pltpu.make_async_copy(src, dst, sems.at[n]) for n, (src, dst) in enumerate(pairs)]
    for copy in copies:
        copy.start()
    return copies


def first_kernel(
    block_hbm, point_hbm, state_hbm, weight_hbm, out_ref, state_ref,
    block_s, point_s, weight_s, pick_s, high_s, low_s, acc_s, sems,
):
    pairs = ((block_hbm, block_s), (point_hbm, point_s), (state_hbm, state_ref), (weight_hbm, weight_s))
    copies = fetch(pairs, sems)
    copies[0].wait()
    copies[1].wait()
    picks(block_s, point_s, pick_s)
    copies[2].wait()
    windows(state_ref, high_s, low_s)
    copies[3].wait()
    gather(pick_s, point_s, weight_s, out_ref, high_s, low_s, acc_s)


def product(a, b):
    total = a[:, 0:1] * b[0:1, :]
    for j in range(1, VARS):
        total = total + a[:, j : j + 1] * b[j : j + 1, :]
    return total


def matrices(inv_ref, low_jac_ref, up_jac_ref, order, wide_ref, maps_ref, native_s, square_s, spread_s, mats_s):
    for i in range(VARS):
        row = inv_ref[i]
        native_s[INV, i] = row
        for which, jac_ref in ((LOW, low_jac_ref), (UP, up_jac_ref)):
            total = row[:, 0:1] * jac_ref[0]
            for j in range(1, VARS):
                total = total + row[:, j : j + 1] * jac_ref[j]
            native_s[which, i] = total
    for which in (INV, LOW, UP):
        for i in range(VARS):
            row = native_s[which, i]
            for j in range(VARS):
                at = ((which * VARS + i) * VARS + j) * BLK
                spread_s[at : at + BLK] = jnp.broadcast_to(row[:, j : j + 1], (BLK, LANES))
    for k in range(BLK):
        wide_ref[k] = spread_s[pl.ds(order[k], 3 * SQUARE, stride=BLK), :]
        for which in (LOW, UP):
            for i in range(VARS):
                square_s[which * BLK + k, i : i + 1, :] = native_s[which, i, pl.ds(order[k], 1), :]
    low = [square_s[LOW * BLK + k] for k in range(BLK)]
    up = [square_s[UP * BLK + k] for k in range(BLK)]
    downs, ups = [low[0]], [up[0]]
    for k in range(1, BLK):
        downs.append(product(low[k], downs[-1]))
        ups.append(product(ups[-1], up[k]))
    mixed = [downs[0]] + [product(ups[k - 1], downs[k]) for k in range(1, BLK)]
    mats_s[...] = jnp.zeros_like(mats_s)
    for m, mat in enumerate([downs[-1], ups[-1]] + mixed):
        mats_s[0:VARS, m * VARS : (m + 1) * VARS] = mat
    mats = mats_s[...]
    for half in range(2):
        line = mats[3 * half : 3 * half + 1]
        for n in (1, 2):
            line = line + pltpu.roll(mats[3 * half + n : 3 * half + n + 1], n * SQUARE, 1)
        maps_ref[6 + half] = jnp.broadcast_to(line, (TILES, LANES))


def residual(state_ref, forcing_ref, visc_ref, count_ref, out_ref):
    count = count_ref[...]
    lane = lax.broadcasted_iota(jnp.int32, (ROWS, LANES), 1)
    row = lax.broadcasted_iota(jnp.int32, (ROWS, LANES), 0)
    for v in range(VARS):
        x = state_ref[v]
        after = pltpu.roll(x, LANES - 1, 1)
        after = jnp.where(lane == LANES - 1, pltpu.roll(after, ROWS - BLK, 0), after)
        after = jnp.where((lane == LANES - 1) & (row >= ROWS - BLK), 0.0, after)
        before = pltpu.roll(x, 1, 1)
        before = jnp.where(lane == 0, pltpu.roll(before, BLK, 0), before)
        before = jnp.where((lane == 0) & (row < BLK), 0.0, before)
        out_ref[v] = forcing_ref[v] + visc_ref[...] * (after - 2.0 * x + before) + (out_ref[v] - count * x)


def turned(x):
    return jnp.concatenate([x[:, :LANES], x[:, LANES:]], axis=0).T


def contract(left, right):
    return lax.dot_general(left, right, (((1,), (1,)), ((), ())), preferred_element_type=F32)


def base_kernel(
    block_hbm, point_hbm, diag_hbm, lowc_hbm, upc_hbm, inv_hbm, low_jac_hbm, up_jac_hbm, order_hbm,
    place_ref, count_ref, wide_ref, factor_ref, maps_ref, point_ref, order_ref,
    block_ref, diag_ref, lowc_ref, upc_ref, inv_ref, low_jac_ref, up_jac_ref,
    left_s, native_s, square_s, spread_s, mats_s, sems,
):
    pairs = (
        (block_hbm, block_ref), (point_hbm, point_ref), (order_hbm, order_ref), (inv_hbm, inv_ref),
        (low_jac_hbm, low_jac_ref), (up_jac_hbm, up_jac_ref), (diag_hbm, diag_ref), (lowc_hbm, lowc_ref),
        (upc_hbm, upc_ref),
    )
    for copy in fetch(pairs, sems):
        copy.wait()
    order = order_of(order_ref)
    for c in range(SLOTS):
        cols = slice(c * LANES, (c + 1) * LANES)
        point = point_ref[c : c + 1]
        place_ref[:, cols] = one_hot(256, window_of(block_ref[c : c + 1], point))
        left_s[:, cols] = one_hot(HALF, point & (HALF - 1))
    matrices(inv_ref, low_jac_ref, up_jac_ref, order, wide_ref, maps_ref, native_s, square_s, spread_s, mats_s)
    down = up = None
    for k in range(BLK):
        rows = pl.ds(order[k], TILES, stride=BLK)
        scale = diag_ref[rows, :]
        fall, rise = scale * lowc_ref[rows, :], upc_ref[rows, :]
        factor_ref[DIAG * BLK + k] = scale
        factor_ref[DOWN * BLK + k] = fall
        factor_ref[RISE * BLK + k] = rise
        down = fall if k == 0 else down * fall
        maps_ref[2 + k] = down if k == 0 else down * up
        up = rise if k == 0 else up * rise
    maps_ref[0] = down
    maps_ref[1] = up
    count_ref[...] = turned(contract(left_s[...], place_ref[...]))


def scatter(got_ref, point_ref, place_ref, out_ref, high_s, low_s, total_s):
    high_s[:LANES] = got_ref[pl.ds(0, LANES, stride=2), :].T
    high_s[LANES:] = got_ref[pl.ds(1, LANES, stride=2), :].T[: VARS * SLOTS - LANES]
    got = high_s[...]
    high = got.astype(BF16).astype(F32)
    high_s[...] = high
    low_s[...] = got - high
    for first in range(0, SLOTS, BATCH):
        parts = []
        for c in range(first, first + BATCH):
            here = lax.broadcasted_iota(jnp.int32, (HALF, LANES), 0) == (point_ref[c : c + 1] & (HALF - 1))
            pieces = []
            for ref in (high_s, low_s):
                for v in range(VARS):
                    pieces.append(jnp.where(here, ref[v * SLOTS + c : v * SLOTS + c + 1], 0.0).astype(BF16))
            parts.append(jnp.concatenate(pieces, axis=0))
        left = jnp.concatenate(parts, axis=1)
        total = contract(left, place_ref[:, first * LANES : (first + BATCH) * LANES])
        if first == 0:
            total_s[...] = total
        else:
            total_s[...] += total
    size = VARS * HALF
    for v in range(VARS):
        added = total_s[v * HALF : (v + 1) * HALF] + total_s[size + v * HALF : size + (v + 1) * HALF]
        out_ref[v] = turned(added)


def apply_block(wide_ref, k, which, xs):
    out = []
    for i in range(VARS):
        at = which * SQUARE + i * VARS
        total = wide_ref[k, at : at + 1] * xs[0]
        for j in range(1, VARS):
            total = total + wide_ref[k, at + j : at + j + 1] * xs[j]
        out.append(total)
    return out


def factor_at(factor_ref, which, k, first):
    return factor_ref[which * BLK + k, first : first + SPAN]


def solve_kernel(full, *refs):
    rows = FULL if full else BARE
    got_ref, point_ref, place_ref, wide_ref, factor_ref, order_ref, count_ref, state_ref, visc_hbm, forcing_hbm = refs[:10]
    refs = refs[10:]
    if full:
        maps_ref, refs = refs[0], refs[1:]
    chunk_ref, z_ref, resid_s, high_s, low_s, total_s, visc_s, forcing_s, sems = refs
    copies = fetch(((visc_hbm, visc_s), (forcing_hbm, forcing_s)), sems)
    order = order_of(order_ref)
    if full:
        maps = maps_ref[...]
        for r in range(FULL - BARE):
            chunk_ref[pl.ds(BARE + r, TILES, stride=rows), :] = maps[r]
    scatter(got_ref, point_ref, place_ref, resid_s, high_s, low_s, total_s)
    for copy in copies:
        copy.wait()
    residual(state_ref, forcing_s, visc_s, count_ref, resid_s)
    for first in range(0, TILES, SPAN):

        def put(r, value):
            chunk_ref[pl.ds(first * rows + r, SPAN, stride=rows), :] = value

        z = None
        for k in range(BLK):
            places = pl.ds(order[k] + BLK * first, SPAN, stride=BLK)
            scale = factor_at(factor_ref, DIAG, k, first)
            solved = [scale * x for x in apply_block(wide_ref, k, INV, [resid_s[j, places, :] for j in range(VARS)])]
            if k > 0:
                fall = factor_at(factor_ref, DOWN, k, first)
                solved = [fall * m + x for m, x in zip(apply_block(wide_ref, k, LOW, z), solved)]
            z = solved
            for i in range(VARS):
                z_ref[k, i, first : first + SPAN] = z[i]
        for i in range(VARS):
            put(i, z[i])
        y = z
        for k in reversed(range(BLK - 1)):
            rise = factor_at(factor_ref, RISE, k, first)
            moved = apply_block(wide_ref, k, UP, y)
            y = [z_ref[k, i, first : first + SPAN] + rise * moved[i] for i in range(VARS)]
        for i in range(VARS):
            put(VARS + i, y[i])


MATS = 6


def columns(mats, cols_ref):
    lane = lax.broadcasted_iota(jnp.int32, mats.shape, 1)
    mats = jnp.where(lane < SQUARE, mats, 0.0)
    packed = mats.astype(BF16).astype(F32)
    rest = mats - packed
    for n in (1, 2):
        part = rest.astype(BF16).astype(F32)
        rest = rest - part
        packed = packed + pltpu.roll(part, n * SQUARE, 1)
    packed = packed.astype(BF16)
    row = lax.broadcasted_iota(jnp.int32, (LANES, LANES), 0)
    row = row - jnp.where(row >= SQUARE, SQUARE, 0) - jnp.where(row >= 2 * SQUARE, SQUARE, 0)
    row = row.astype(F32).astype(BF16)
    for m in range(MATS):
        copies = [
            jnp.where(row == jnp.asarray(m * VARS + j, BF16), jnp.ones((), BF16), jnp.zeros((), BF16)) for j in range(VARS)
        ]
        spread = jnp.dot(packed, jnp.concatenate(copies, axis=1), preferred_element_type=F32)
        cols_ref[:, m * VARS * LANES : (m + 1) * VARS * LANES] = spread


def first_chain_kernel(coef_ref, out_ref, cols_ref, value_s, mid_s, mats_s):
    for half in range(2):
        lines = coef_ref[pl.ds(FULL - 2 + half, TILES, stride=FULL), :]
        for n in range(3):
            shifted = pltpu.roll(lines, LANES - n * SQUARE, 1) if n else lines
            mats_s[pl.ds(3 * half + n, TILES, stride=8), :] = shifted
    for i in (VARS, VARS + 1):
        mats_s[pl.ds(i, TILES, stride=8), :] = jnp.zeros((TILES, LANES), F32)
    columns(mats_s[...], cols_ref)
    chain(FULL, coef_ref, coef_ref, cols_ref, out_ref, value_s, mid_s)


def second_chain_kernel(in_ref, coef_ref, cols_ref, out_ref, value_s, mid_s):
    chain(BARE, in_ref, coef_ref, cols_ref, out_ref, value_s, mid_s)


def chain(rows, in_ref, coef_ref, cols_ref, out_ref, value_s, mid_s):
    for i in range(VARS):
        value_s[pl.ds(i, TILES, stride=8), :] = in_ref[pl.ds(i, TILES, stride=rows), :]
        mid_s[pl.ds(i, TILES, stride=8), :] = in_ref[pl.ds(VARS + i, TILES, stride=rows), :]

    def apply(here, m, x):
        terms = []
        for j in range(VARS):
            at = (m * VARS + j) * LANES
            terms.append(cols_ref[here, at : at + LANES] * x[j])
        return ((terms[0] + terms[1]) + (terms[2] + terms[3])) + (terms[4] + terms[5])

    def spread(x):
        return [jnp.broadcast_to(x[j : j + 1], (VARS, LANES)) for j in range(VARS)]

    def coef(s, r):
        return coef_ref[FULL * s + BARE + r : FULL * s + BARE + r + 1]

    down = jnp.zeros((VARS, LANES), F32)
    for s in range(TILES):
        here = slice(8 * s, 8 * s + VARS)
        parts = spread(down)
        mid = mid_s[here]
        for k in range(BLK):
            mid = mid + coef(s, 2 + k) * apply(here, 2 + k, parts)
        mid_s[here] = mid
        after = coef(s, 0) * apply(here, 0, parts) + value_s[here]
        value_s[here] = down
        down = after
    up = jnp.zeros((VARS, LANES), F32)
    for s in reversed(range(TILES)):
        here = slice(8 * s, 8 * s + VARS)
        after = coef(s, 1) * apply(here, 1, spread(up)) + mid_s[here]
        mid_s[here] = up
        up = after
    for i in range(VARS):
        out_ref[pl.ds(i, TILES, stride=BARE), :] = value_s[pl.ds(i, TILES, stride=8), :]
        out_ref[pl.ds(VARS + i, TILES, stride=BARE), :] = mid_s[pl.ds(i, TILES, stride=8), :]


def finish(back_ref, z_ref, state_ref, wide_ref, factor_ref, order_ref, new_ref, corr_ref, star_s, ready=None):
    order = order_of(order_ref)
    for first in range(0, TILES, SPAN):
        here = slice(first, first + SPAN)
        enter = [back_ref[pl.ds(first * BARE + i, SPAN, stride=BARE), :] for i in range(VARS)]
        for k in range(BLK):
            fall = factor_at(factor_ref, DOWN, k, first)
            enter = [fall * m for m in apply_block(wide_ref, k, LOW, enter)]
            for i in range(VARS):
                star_s[k, i, here] = enter[i] + z_ref[k, i, here]
        corr = [back_ref[pl.ds(first * BARE + VARS + i, SPAN, stride=BARE), :] for i in range(VARS)]
        for k in reversed(range(BLK)):
            rise = factor_at(factor_ref, RISE, k, first)
            moved = apply_block(wide_ref, k, UP, corr)
            corr = [star_s[k, i, here] + rise * moved[i] for i in range(VARS)]
            places = pl.ds(order[k] + BLK * first, SPAN, stride=BLK)
            for i in range(VARS):
                if corr_ref is not None:
                    corr_ref[i, places, :] = corr[i]
                new_ref[i, places, :] = state_ref[i, places, :] + corr[i]
        if ready is not None:
            ready(first)


def last_kernel(
    back_ref, z_ref, state_ref, wide_ref, factor_ref, order_ref, new_hbm, corr_hbm, star_s, new_s, corr_s, sems
):
    copies = []

    def ready(first):
        rows = pl.ds(first * BLK, SPAN * BLK)
        for src, dst in ((new_s, new_hbm), (corr_s, corr_hbm)):
            copy = pltpu.make_async_copy(src.at[:, rows, :], dst.at[:, rows, :], sems.at[len(copies)])
            copy.start()
            copies.append(copy)

    finish(back_ref, z_ref, state_ref, wide_ref, factor_ref, order_ref, new_s, corr_s, star_s, ready)
    for copy in copies:
        copy.wait()


def middle_kernel(
    back_ref, z_ref, state_ref, wide_ref, factor_ref, order_ref, block_hbm, point_hbm, weight_hbm, new_ref, out_ref,
    star_s, block_s, point_s, weight_s, pick_s, high_s, low_s, acc_s, sems,
):
    copies = fetch(((block_hbm, block_s), (point_hbm, point_s), (weight_hbm, weight_s)), sems)
    finish(back_ref, z_ref, state_ref, wide_ref, factor_ref, order_ref, new_ref, None, star_s)
    windows(new_ref, high_s, low_s)
    for copy in copies:
        copy.wait()
    picks(block_s, point_s, pick_s)
    gather(pick_s, point_s, weight_s, out_ref, high_s, low_s, acc_s)


def shape(*dims, dtype=F32):
    return pltpu.VMEM(dims, dtype)


def call(kernel, name, outs, operands, scratch=(), outside=(), beside=False, out_space=pltpu.VMEM):
    spaces = [pltpu.HBM if n in outside else pltpu.VMEM for n in range(len(operands))]
    return pl.pallas_call(
        kernel,
        out_shape=outs,
        in_specs=[pl.BlockSpec(memory_space=space) for space in spaces],
        out_specs=[pl.BlockSpec(memory_space=out_space)] * len(outs),
        scratch_shapes=list(scratch),
        compiler_params=PARAMS,
        cost_estimate=BESIDE if beside else None,
        name=name,
    )(*[pltpu.with_memory_space_constraint(x, pltpu.HBM) if n in outside else x for n, x in enumerate(operands)])


def exchange(x, axes, count):
    parts = x.reshape(count, 1, -1)
    return lax.all_to_all(parts, axes, split_axis=0, concat_axis=0, tiled=True).reshape(x.shape)


def per_device(
    state, forcing, viscosity, inverses, lower_jac, upper_jac, diag_scale, lower_coupling, upper_coupling,
    donor_block, donor_point, donor_weight, fringe_block, fringe_point, block_order,
):
    big = (VARS, ROWS, LANES)
    state, forcing = to_rows(state[0]), to_rows(forcing[0])
    visc, diag, lowc, upc = (field_rows(x[0]) for x in (viscosity, diag_scale, lower_coupling, upper_coupling))
    inv, low_jac, up_jac = (x[0].transpose(1, 0, 2) for x in (inverses, lower_jac, upper_jac))
    src_block, src_point, dst_block, dst_point = (x[0].T for x in (donor_block, donor_point, fringe_block, fringe_point))
    weight = donor_weight[0].transpose(1, 2, 0)
    sent = VARS * (HALF + TAIL)
    gather_scratch = [pltpu.VMEM((sent, 256), BF16), pltpu.VMEM((sent, 256), BF16), pltpu.VMEM((256, LANES), F32)]
    star_scratch = [pltpu.VMEM((BLK, VARS, TILES, LANES), F32)]
    chain_scratch = [pltpu.VMEM((TILES * 8, LANES), F32) for _ in range(3)]
    dma = pltpu.SemaphoreType.DMA

    def alike(x):
        return pltpu.VMEM(x.shape, x.dtype)

    source = (src_block, src_point, weight)
    source_scratch = [alike(x) for x in source] + [pltpu.VMEM((256, SLOTS * LANES), BF16)] + gather_scratch
    solve_scratch = [
        pltpu.VMEM(big, F32),
        pltpu.VMEM((VARS * SLOTS, LANES), F32),
        pltpu.VMEM((VARS * SLOTS, LANES), F32),
        pltpu.VMEM((2 * VARS * HALF, 256), F32),
        alike(visc),
        alike(forcing),
        dma((2,)),
    ]
    interp, state = call(
        first_kernel,
        "first",
        [shape(256, LANES), shape(*big)],
        (src_block, src_point, state, weight),
        source_scratch + [dma((4,))],
        outside=range(4),
    )
    got = exchange(interp, ("sweep", "grp"), 128)
    place, count, wide, factors, maps, dst_point, block_order = call(
        base_kernel,
        "base",
        [
            shape(256, SLOTS * LANES, dtype=BF16),
            shape(ROWS, LANES),
            shape(BLK, 3 * SQUARE, LANES),
            shape(3 * BLK, TILES, LANES),
            shape(FULL - BARE, TILES, LANES),
            alike(dst_point),
            alike(block_order),
        ],
        (dst_block, dst_point, diag, lowc, upc, inv, low_jac, up_jac, block_order),
        [alike(x) for x in (dst_block, diag, lowc, upc, inv, low_jac, up_jac)]
        + [
            pltpu.VMEM((HALF, SLOTS * LANES), BF16),
            pltpu.VMEM((3, VARS, BLK, VARS), F32),
            pltpu.VMEM((3 * BLK, VARS, VARS), F32),
            pltpu.VMEM((3 * SQUARE * BLK + 8 * BLK, LANES), F32),
            pltpu.VMEM((8, LANES), F32),
            dma((9,)),
        ],
        outside=range(9),
        beside=True,
    )

    def solve(full, got, state):
        operands = (got, dst_point, place, wide, factors, block_order, count, state, visc, forcing)
        operands += (maps,) if full else ()
        rows = FULL if full else BARE
        outs = [shape(TILES * rows, LANES), shape(BLK, VARS, TILES, LANES)]
        return call(lambda *refs: solve_kernel(full, *refs), "solve", outs, operands, solve_scratch, outside=(8, 9))

    chunk, z = solve(True, got, state)
    coefs = exchange(chunk, "sweep", TILES)
    entering, cols = call(
        first_chain_kernel,
        "chain",
        [shape(TILES * BARE, LANES), shape(TILES * 8, MATS * VARS * LANES)],
        (coefs,),
        chain_scratch,
    )
    back = exchange(entering, "sweep", TILES)
    state, interp = call(
        middle_kernel,
        "middle",
        [shape(*big), shape(256, LANES)],
        (back, z, state, wide, factors, block_order) + source,
        star_scratch + source_scratch + [dma((3,))],
        outside=(6, 7, 8),
    )
    got = exchange(interp, ("sweep", "grp"), 128)
    chunk, z = solve(False, got, state)
    values = exchange(chunk, "sweep", TILES)
    (entering,) = call(
        second_chain_kernel, "chain", [shape(TILES * BARE, LANES)], (values, coefs, cols), chain_scratch[:2]
    )
    back = exchange(entering, "sweep", TILES)
    state, correction = call(
        last_kernel,
        "last",
        [jax.ShapeDtypeStruct(big, F32)] * 2,
        (back, z, state, wide, factors, block_order),
        star_scratch + [pltpu.VMEM(big, F32), pltpu.VMEM(big, F32), dma((2 * TILES // SPAN,))],
        out_space=pltpu.HBM,
    )
    return from_rows(state)[None], from_rows(correction)[None]


def solution(mesh):
    blocks = P("grp", "sweep", None, None)
    field = P("grp", "sweep", None)
    table = P(("sweep", "grp"), None, None)
    return jax.shard_map(
        per_device,
        mesh=mesh,
        in_specs=(
            blocks, blocks, field, blocks, blocks, blocks, field, field, field,
            table, table, P(("sweep", "grp"), None, None, None), table, table, P("grp", "sweep"),
        ),
        out_specs=(blocks, blocks),
        check_vma=False,
    )
```
